256 devices in a mesh: band: 8 (over x, core), tile: 32 (over y, z).
Axes of the slice: x: 4, y: 4, z: 8, core: 2. Of those that a mesh axis runs over, the one named last changes fastest.
Arguments:
- wind_read: bfloat16 [8, 128, 8192], P(None, 'band', 'tile'), may hold values from -4 to 4
- temp_read: bfloat16 [8, 128, 8192], P(None, 'band', 'tile'), may hold values from 0.69921875 to 1.296875
- diff_read: bfloat16 [8, 128, 8192], P(None, 'band', 'tile'), may hold values from 0.1 to 8400
- removal_read: bfloat16 [8, 128, 8192], P(None, 'band', 'tile'), may hold values from 0.049804688 to 0.5
- frac: float32 [40960, 128], P(('band', 'tile')), may hold values from 0 to 1
- height: float32 [40960, 128], P(('band', 'tile')), may hold values from 0 to 127
- mass: float32 [40960, 128], P(('band', 'tile')), may hold values from 0.5 to 2
- noise: float32 [40960, 128], P(('band', 'tile')), may hold values from -5 to 5
- column: int32 [40960, 128], P(('band', 'tile')), may hold values from 0 to 255
- dest: int32 [40960], P(('band', 'tile')), may hold values from 0 to 31, as said below
Outputs:
- concentration: float32 [8, 128, 8192], P('band', None, 'tile')
- moved_height: float32 [81920, 128], P(('band', 'tile'))
The draws below stay inside these ranges and needn't reach their ends.
Inputs may be any that keep to these rules, and one draw needn't show every extreme that they name: `dest`: among the 160 blocks of one device no tile is named by more than 10; in every band one tile is named by exactly 10 blocks of every device of the band.
All inputs are finite; a program needn't handle non-finite values.
Results may differ from the reference program's by a relative error of at most 0.0045.
Values may be sent and summed in bfloat16 or wider, within the bound.
A program may use at most 64 MiB of HBM per device.

```python
import math
import jax
import jax.numpy as jnp
from jax import lax

LEV = 128
COLS = 256
PB = 128
B_DEV = 160
NBLK = 40960
N_BAND = 8
N_TILE = 32


def draw_dest(key, part):
    cap = 2 * B_DEV // N_TILE
    hot = jax.random.randint(jax.random.fold_in(key, 11), (N_BAND,), 0, N_TILE).astype(jnp.int32)
    hot_dev = jnp.repeat(hot, N_TILE)
    pool = (jnp.arange((N_TILE - 1) * cap, dtype=jnp.int32) // cap).astype(jnp.int32)
    keys = jax.random.split(jax.random.fold_in(key, 12), N_BAND * N_TILE)

    def one_device(dev_key, hot_tile):
        first_key, second_key = jax.random.split(dev_key)
        picked = jax.random.permutation(first_key, pool)[:B_DEV - cap]
        picked = (picked + hot_tile + 1) % N_TILE
        full = jnp.concatenate([jnp.full((cap,), hot_tile, jnp.int32), picked.astype(jnp.int32)])
        return jax.random.permutation(second_key, full)
    return jax.vmap(one_device)(keys, hot_dev).reshape(-1).astype(jnp.int32)


def draw_diff_read(key, part):
    key = jax.random.fold_in(key, 21)
    base_key, pick_key, factor_key, rough_key = jax.random.split(key, 4)
    shape = (N_BAND, LEV, N_TILE * COLS)
    column_shape = (N_BAND, 1, N_TILE * COLS)
    base = jnp.exp(jax.random.uniform(base_key, shape, jnp.float32, math.log(0.1), math.log(2.0)))
    pick = jax.random.uniform(pick_key, column_shape, jnp.float32, 0.0, 1.0)
    factor = jnp.exp(jax.random.uniform(factor_key, column_shape, jnp.float32, math.log(2000.0), math.log(6000.0)))
    rough = jax.random.uniform(rough_key, shape, jnp.float32, 0.6, 1.4)
    share = 0.15
    field = jnp.where(pick < share, factor * rough, base)
    return field.astype(jnp.float32).astype(jnp.bfloat16)


def with_ends(result, own_key, least, top_value):
    longest = result.shape.index(max(result.shape))
    spots = []
    for shift in (0, 1):
        where = [jax.random.randint(jax.random.fold_in(own_key, axis), (), 0, length) for axis, length in enumerate(result.shape)]
        where[longest] = (where[longest] + shift) % result.shape[longest]
        spots.append(tuple(where))
    return result.at[spots[0]].set(least).at[spots[1]].set(top_value)


def levels(key, shape, cuts, least, high):
    factor_of = 1.0
    for axis_at, shards_of in cuts:
        heights = jax.random.uniform(jax.random.fold_in(jax.random.fold_in(key, 6), axis_at), (shards_of,), jnp.float32, least / len(cuts), high / len(cuts))
        factor_of = factor_of * jnp.repeat(jnp.exp(heights), shape[axis_at] // shards_of).reshape((-1,) + (1,) * (len(shape) - 1 - axis_at))
    return factor_of


def bell_draw(stream_key, shape, deviation, reach, pieces=(), kind=jnp.bfloat16):
    array = jax.random.normal(stream_key, shape, jnp.float32) * deviation
    if len(pieces) > 0:
        array = levels(stream_key, shape, pieces, -0.22, 0.18) * array
    return jnp.clip(array, min=-reach, max=reach).astype(kind)


def setup_inputs(seed: int = 0) -> dict:
    streams_of = jax.random.split(jax.random.key(seed), 11)
    return {
        "wind_read": bell_draw(streams_of[0], (N_BAND, LEV, N_TILE * COLS), 1.0, 4.0, ((1, 8), (2, 32))),
        "temp_read": jnp.clip(0.69921875 + 0.59765625 * jax.random.uniform(streams_of[1], (N_BAND, LEV, N_TILE * COLS), jnp.float32) ** levels(streams_of[1], (N_BAND, LEV, N_TILE * COLS), ((1, 8), (2, 32)), -0.2, 0.2), 0.69921875, 1.296875).astype(jnp.bfloat16),
        "diff_read": draw_diff_read(jax.random.fold_in(streams_of[10], 71), 0),
        "removal_read": jnp.clip(jnp.exp(math.log(0.5) - 2.306499 * jax.random.uniform(streams_of[3], (N_BAND, LEV, N_TILE * COLS), jnp.float32) ** levels(streams_of[3], (N_BAND, LEV, N_TILE * COLS), ((1, 8), (2, 32)), -0.2, 0.2)), 0.049804688, 0.5).astype(jnp.bfloat16),
        "frac": jnp.clip(1.0 * jax.random.uniform(streams_of[4], (NBLK, PB), jnp.float32) ** levels(streams_of[4], (NBLK, PB), ((0, 256),), -0.2, 0.2), 0.0, 1.0),
        "height": jnp.clip(127.0 * jax.random.uniform(streams_of[5], (NBLK, PB), jnp.float32) ** levels(streams_of[5], (NBLK, PB), ((0, 256),), -0.2, 0.2), 0.0, 127.0),
        "mass": jnp.clip(jnp.exp(math.log(2.0) - 1.3862944 * jax.random.uniform(streams_of[6], (NBLK, PB), jnp.float32) ** levels(streams_of[6], (NBLK, PB), ((0, 256),), -0.2, 0.2)), 0.5, 2.0),
        "noise": bell_draw(streams_of[7], (NBLK, PB), 1.0, 5.0, ((0, 256),), jnp.float32),
        "column": with_ends(jax.random.randint(streams_of[8], (NBLK, PB), 0, COLS), jax.random.fold_in(streams_of[8], 1), 0, COLS - 1).astype(jnp.int32),
        "dest": draw_dest(jax.random.fold_in(streams_of[10], 71), 0),
    }


def implicit_diffusion(binned, kdiff):
    kappa = 0.5 * (kdiff[:-1] + kdiff[1:])
    zero_row = jnp.zeros_like(kdiff[:1])
    upper = jnp.concatenate([kappa, zero_row], axis=0)
    lower = jnp.concatenate([zero_row, kappa], axis=0)
    diag = 1.0 + upper + lower

    def forward(carry, inputs):
        prev_c, prev_d = carry
        sub, mid, sup, rhs = inputs
        pivot = mid - sub * prev_c
        new_c = sup / pivot
        new_d = (rhs - sub * prev_d) / pivot
        return ((new_c, new_d), (new_c, new_d))
    start = jnp.zeros_like(binned[0])
    _, (coef_c, coef_d) = lax.scan(forward, (start, start), (-lower, diag, -upper, binned))

    def backward(carry, inputs):
        cval, dval = inputs
        value = dval - cval * carry
        return (value, value)
    _, solved = lax.scan(backward, start, (coef_c, coef_d), reverse=True)
    return solved

def build_send(records, dest):
    cap = 2 * B_DEV // N_TILE
    onehot = (dest[:, None] == jnp.arange(N_TILE, dtype=jnp.int32)[None, :]).astype(jnp.int32)
    before = jnp.cumsum(onehot, axis=0) - onehot
    rank = lax.optimization_barrier(jnp.sum(before * onehot, axis=1)).astype(jnp.int32)
    slot = (dest * cap + rank).astype(jnp.int32)
    empty = jnp.zeros((N_TILE * cap, 5, PB), jnp.float32)
    return empty.at[slot].set(records)

def owner_work(received, table, east):
    frac_r = received[:, 0].reshape(-1)
    height_r = received[:, 1].reshape(-1)
    mass_r = received[:, 2].reshape(-1)
    noise_r = received[:, 3].reshape(-1)
    col = received[:, 4].reshape(-1).astype(jnp.int32)
    extended = jnp.concatenate([table, east[:, None]], axis=1).astype(jnp.float32)
    left = (1.0 - frac_r).astype(jnp.bfloat16).astype(jnp.float32)
    right = frac_r.astype(jnp.bfloat16).astype(jnp.float32)
    horiz = extended[:, col] * left[None, :] + extended[:, col + 1] * right[None, :]
    horiz = horiz.reshape(4, LEV, -1)
    low = jnp.clip(jnp.floor(height_r), 0, LEV - 2).astype(jnp.int32)
    frac_z = height_r - low.astype(jnp.float32)
    pick_lo = jnp.take_along_axis(horiz, low[None, None, :], axis=1)[:, 0]
    pick_hi = jnp.take_along_axis(horiz, (low + 1)[None, None, :], axis=1)[:, 0]
    value = pick_lo * (1.0 - frac_z)[None] + pick_hi * frac_z[None]
    znew = jnp.clip(height_r + value[0] + jnp.sqrt(2.0 * value[2]) * noise_r, 0.0, LEV - 1.0)
    moved = jnp.where(mass_r > 0, znew, 0.0)
    load = mass_r * jnp.exp(-value[3]) * value[1]
    low_new = jnp.clip(jnp.floor(znew), 0, LEV - 2).astype(jnp.int32)
    frac_new = znew - low_new.astype(jnp.float32)
    load_lo = (load * (1.0 - frac_new)).astype(jnp.bfloat16).astype(jnp.float32)
    load_hi = (load * frac_new).astype(jnp.bfloat16).astype(jnp.float32)
    binned = jnp.zeros((LEV, COLS), jnp.float32)
    binned = binned.at[low_new, col].add(load_lo).at[low_new + 1, col].add(load_hi)
    kdiff = table.reshape(4, LEV, COLS)[2].astype(jnp.float32)
    conc = implicit_diffusion(binned, kdiff)
    return (conc, moved.reshape(-1, PB))

def reference(wind_read, temp_read, diff_read, removal_read, frac, height, mass, noise, column, dest):
    fields = jnp.stack([wind_read, temp_read, diff_read, removal_read])
    fields = fields.reshape(4, N_BAND, LEV, N_TILE, COLS).transpose(1, 3, 0, 2, 4)
    tables = fields.reshape(N_BAND, N_TILE, 4 * LEV, COLS)
    easts = jnp.roll(tables[:, :, :, 0], -1, axis=1)
    records = jnp.stack([frac, height, mass, noise, column.astype(jnp.float32)], axis=1)
    records = records.reshape(N_BAND * N_TILE, B_DEV, 5, PB)
    dests = dest.reshape(N_BAND * N_TILE, B_DEV)
    sends = jax.vmap(build_send)(records, dests)
    cap = 2 * B_DEV // N_TILE
    sends = sends.reshape(N_BAND, N_TILE, N_TILE, cap, 5, PB).transpose(0, 2, 1, 3, 4, 5)
    received = sends.reshape(N_BAND * N_TILE, N_TILE * cap, 5, PB)
    tables = tables.reshape(N_BAND * N_TILE, 4 * LEV, COLS)
    easts = easts.reshape(N_BAND * N_TILE, 4 * LEV)
    conc, moved = lax.map(lambda item: owner_work(item[0], item[1], item[2]), (received, tables, easts))
    conc = conc.reshape(N_BAND, N_TILE, LEV, COLS).transpose(0, 2, 1, 3).reshape(N_BAND, LEV, N_TILE * COLS)
    return (conc, moved.reshape(-1, PB))
```

```python
import jax
import jax.numpy as jnp
from jax import lax
from jax.experimental import pallas as pl
from jax.experimental.pallas import tpu as pltpu
from jax.sharding import PartitionSpec as P

LEV = 128
COLS = 256
CAP = 10
PB = 128
CH = 2
F32 = jnp.float32
BF = jnp.bfloat16


def iota(shape, dim, dtype=F32):
    return lax.broadcasted_iota(jnp.int32, shape, dim).astype(dtype)


def split_levels(table_ref, tperm_ref):
    row = lax.broadcasted_iota(jnp.int32, (LEV, LEV), 0)
    col = lax.broadcasted_iota(jnp.int32, (LEV, LEV), 1)
    source = jnp.where(row < LEV // 2, 2 * row, 2 * row - (LEV - 1))
    perm = (col == source).astype(F32).astype(BF)
    for f in range(4):
        part = pl.ds(f * LEV, LEV)
        tperm_ref[part, :] = jnp.dot(perm, table_ref[part, :], preferred_element_type=F32).astype(BF)


def set_kappa(table_ref, upper_ref, lower_ref):
    k = table_ref[pl.ds(2 * LEV, LEV), :].astype(F32)
    kappa = 0.5 * (k[:-1] + k[1:])
    zero = jnp.zeros((1, COLS), F32)
    upper_ref[...] = jnp.concatenate([kappa, zero], axis=0)
    lower_ref[...] = jnp.concatenate([zero, kappa], axis=0)


def pivots(step, carry, upper_ref, lower_ref, inv_ref):
    top, bot = carry
    for i in range(2):
        k = 2 * step + i
        u = upper_ref[pl.ds(k, 1), :]
        inv = 1.0 / (top + u)
        inv_ref[pl.ds(k, 1), :] = inv
        last_top = top
        top = 1.0 + u * (top * inv)
        m = LEV - 1 - k
        low = lower_ref[pl.ds(m, 1), :]
        inv = 1.0 / (bot + low)
        inv_ref[pl.ds(m, 1), :] = inv
        last_bot = bot
        bot = 1.0 + low * (bot * inv)
    return (top, bot), (last_top, last_bot)


def interpolate(fr, height, col, tperm_ref, val_ref):
    left = (1.0 - fr)
    low = jnp.clip(jnp.floor(height), 0.0, LEV - 2.0)
    odd_i = jnp.floor(low * 0.5)
    even_i = jnp.floor((low + 1.0) * 0.5)
    w_even = jnp.maximum(0.0, 1.0 - jnp.abs(height - 2.0 * even_i))
    w_odd = jnp.maximum(0.0, 1.0 - jnp.abs(height - (2.0 * odd_i + 1.0)))
    g_even = jnp.floor(even_i * 0.125)
    g_odd = jnp.floor(odd_i * 0.125)
    s_even = even_i - 8.0 * g_even
    s_odd = odd_i - 8.0 * g_odd
    ids = iota((COLS, PB), 0, BF)
    sub = iota((8, PB), 0)
    zero = jnp.zeros((COLS, PB), BF)

    def spread(x, c, rows, dtype=F32):
        return jnp.broadcast_to(x[c:c + 1], (rows, PB)).astype(dtype)

    for c0 in range(0, CAP, CH):
        weights = []
        for c in range(c0, c0 + CH):
            cb = spread(col, c, COLS, BF)
            cb1 = spread(col + 1.0, c, COLS, BF)
            lb = spread(left, c, COLS, BF)
            rb = spread(fr, c, COLS, BF)
            weights.append(jnp.where(ids == cb, lb, jnp.where(ids == cb1, rb, zero)))
        horiz = jnp.dot(tperm_ref[...], jnp.concatenate(weights, axis=1), preferred_element_type=F32)
        for i in range(CH):
            c = c0 + i
            ge = spread(g_even, c, 8)
            go = spread(g_odd, c, 8)
            we = jnp.where(sub == spread(s_even, c, 8), spread(w_even, c, 8), 0.0)
            wo = jnp.where(sub == spread(s_odd, c, 8), spread(w_odd, c, 8), 0.0)
            e_masks = [ge >= float(g) for g in range(1, 8)]
            o_masks = [go >= float(g) for g in range(1, 8)]
            lanes = slice(i * PB, (i + 1) * PB)
            for f in range(4):
                base = f * LEV
                e = horiz[base:base + 8, lanes]
                o = horiz[base + 64:base + 72, lanes]
                for g in range(1, 8):
                    e = jnp.where(e_masks[g - 1], horiz[base + 8 * g:base + 8 * g + 8, lanes], e)
                    o = jnp.where(o_masks[g - 1], horiz[base + 64 + 8 * g:base + 72 + 8 * g, lanes], o)
                val_ref[f, c:c + 1, :] = jnp.sum(e * we + o * wo, axis=0, keepdims=True)


def move(fr, height, noise, mass, col, val, east):
    low = jnp.clip(jnp.floor(height), 0.0, LEV - 2.0)
    fz = height - low
    right = fr.astype(BF).astype(F32)
    edge = jnp.where(col == COLS - 1.0, right, 0.0)
    low_i = low.astype(jnp.int32)
    pad = jnp.zeros((16 - CAP, PB), jnp.int32)
    low_p = jnp.concatenate([low_i, pad], axis=0)
    out = []
    for f in range(4):
        lo = jnp.concatenate([jnp.take_along_axis(east[f], low_p[r:r + 8], axis=1) for r in (0, 8)], axis=0)[:CAP]
        hi = jnp.concatenate([jnp.take_along_axis(east[f], low_p[r:r + 8] + 1, axis=1) for r in (0, 8)], axis=0)[:CAP]
        out.append(val[f] + edge * (lo * (1.0 - fz) + hi * fz))
    w, temp, kd, rate = out
    znew = jnp.clip(height + w + jnp.sqrt(2.0 * kd) * noise, 0.0, LEV - 1.0)
    moved = jnp.where(mass > 0, znew, 0.0)
    load = mass * jnp.exp(-rate) * temp
    low = jnp.clip(jnp.floor(znew), 0.0, LEV - 2.0)
    fz = znew - low
    return moved, low, load * (1.0 - fz), load * fz


def binning(low, load_lo, load_hi, col):
    lev = iota((LEV, PB), 0, BF)
    ids = iota((COLS, PB), 0, BF)
    one = jnp.ones((COLS, PB), BF)
    loads, picks = [], []
    for c in range(CAP):
        lb = jnp.broadcast_to(low[c:c + 1], (LEV, PB)).astype(BF)
        hb = jnp.broadcast_to(low[c:c + 1] + 1.0, (LEV, PB)).astype(BF)
        a = jnp.broadcast_to(load_lo[c:c + 1], (LEV, PB)).astype(BF)
        b = jnp.broadcast_to(load_hi[c:c + 1], (LEV, PB)).astype(BF)
        loads.append(jnp.where(lev == lb, a, jnp.where(lev == hb, b, jnp.zeros_like(a))))
        cb = jnp.broadcast_to(col[c:c + 1], (COLS, PB)).astype(BF)
        picks.append(jnp.where(ids == cb, one, jnp.zeros_like(one)))
    return lax.dot_general(jnp.concatenate(picks, axis=1), jnp.concatenate(loads, axis=1),
                           (((1,), (1,)), ((), ())), preferred_element_type=F32)


def solve(ends, binned, upper_ref, lower_ref, inv_ref, rhs_ref, fwd_ref, back_ref, out_ref):
    top, bot = ends
    half = LEV // 2
    inv = inv_ref[...]
    u, low = upper_ref[...], lower_ref[...]
    upper_rows = lax.broadcasted_iota(jnp.int32, (LEV, COLS), 0) < half
    rhs_ref[...] = binned * inv
    fwd_ref[...] = jnp.where(upper_rows, low, u) * inv
    back_ref[...] = jnp.where(upper_rows, u, low) * inv
    d = rhs_ref[0:1, :]
    e = rhs_ref[LEV - 1:LEV, :]
    ds, es = [d], [e]
    for k in range(1, half):
        m = LEV - 1 - k
        d = rhs_ref[k:k + 1, :] + fwd_ref[k:k + 1, :] * d
        e = rhs_ref[m:m + 1, :] + fwd_ref[m:m + 1, :] * e
        ds.append(d)
        es.append(e)
    kappa = upper_ref[half - 1:half, :]
    alpha = back_ref[half - 1:half, :]
    beta = back_ref[half:half + 1, :]
    det = (kappa * (top + bot) + top * bot) * inv_ref[half - 1:half, :] * inv_ref[half:half + 1, :]
    x = (d + alpha * e) / det
    y = e + beta * x
    out_ref[half - 1:half, :] = x
    out_ref[half:half + 1, :] = y
    for k in range(half - 2, -1, -1):
        m = LEV - 1 - k
        x = ds[k] + back_ref[k:k + 1, :] * x
        y = es[k] + back_ref[m:m + 1, :] * y
        out_ref[k:k + 1, :] = x
        out_ref[m:m + 1, :] = y


N_BAND = 8
N_TILE = 32
NY, NZ = 4, 8
B_DEV = 160
SUB = LEV // N_BAND
ROWS = 4 * CAP


def offset(i):
    q, dy = i // NY, i % NY
    dz = ((q + 1) // 2) * (q % 2) + ((NZ - q // 2) % NZ) * (1 - q % 2)
    return dy, dz


def place(tile, i, sign):
    dy, dz = offset(i)
    y = (tile // NZ + NY + sign * dy) % NY
    z = (tile % NZ + NZ + sign * dz) % NZ
    return y * NZ + z


def build(dest_ref, parts, col_ref, send_f, send_c):
    dest = dest_ref[...].astype(F32)
    wide = jnp.broadcast_to(dest, (B_DEV, B_DEV))
    row = lax.broadcasted_iota(jnp.int32, (B_DEV, B_DEV), 0)
    lane = lax.broadcasted_iota(jnp.int32, (B_DEV, B_DEV), 1)
    tall = jnp.sum(jnp.where(row == lane, wide, 0.0), axis=1, keepdims=True)
    same = jnp.where((tall == wide) & (row < lane), 1.0, 0.0)
    rank = jnp.sum(same, axis=0, keepdims=True)
    slots = N_TILE * CAP
    pick = jnp.where(iota((slots, B_DEV), 0) == dest * CAP + rank, 1.0, 0.0).astype(BF)
    for f, ref in enumerate(parts):
        x = ref[...]
        hi = x.astype(BF)
        rest = x - hi.astype(F32)
        mid = rest.astype(BF)
        low = (rest - mid.astype(F32)).astype(BF)
        total = jnp.dot(pick, hi, preferred_element_type=F32)
        total = total + jnp.dot(pick, mid, preferred_element_type=F32)
        total = total + jnp.dot(pick, low, preferred_element_type=F32)
        send_f[pl.ds(f, slots, stride=4), :] = total
    pick = jnp.where(iota((N_TILE * 16, B_DEV), 0) == dest * 16 + rank, 1.0, 0.0).astype(BF)
    cols = jnp.dot(pick, col_ref[...].astype(F32).astype(BF), preferred_element_type=F32)
    send_c[...] = cols.astype(BF).reshape(N_TILE, 16, PB)


def kernel(wind, temp, diff, removal, frac, height, noise, mass, column, dest,
           conc_ref, moved_ref,
           table, tperm, east_out, east_in, send_f, send_c, recv_f, recv_c,
           val, binned, upper, lower, inv, rhs, fwd, back,
           field_send, field_recv, own_sem, east_sems, f_send, f_recv, c_send, c_recv):
    band, tile = lax.axis_index("band"), lax.axis_index("tile")
    barrier = pltpu.get_barrier_semaphore()

    def greet_tile(i, _):
        pl.semaphore_signal(barrier, inc=1, device_id=(band, place(tile, i, 1)), device_id_type=pl.DeviceIdType.MESH)
        return 0

    def greet_band(i, _):
        pl.semaphore_signal(barrier, inc=1, device_id=((band + i) % N_BAND, tile), device_id_type=pl.DeviceIdType.MESH)
        return 0

    lax.fori_loop(1, N_TILE, greet_tile, 0)
    lax.fori_loop(1, N_BAND, greet_band, 0)
    fields = (wind, temp, diff, removal)
    own = [pltpu.make_async_copy(ref.at[band], table.at[pl.ds(pl.multiple_of(f * LEV + band * SUB, SUB), SUB)], own_sem.at[f])
           for f, ref in enumerate(fields)]
    for copy in own:
        copy.start()
    build(dest, (frac, height, noise, mass), column, send_f, send_c)
    pl.semaphore_wait(barrier, N_TILE + N_BAND - 2)

    def field_copy(i, f, to, rows_of):
        return pltpu.make_async_remote_copy(
            src_ref=fields[f].at[to], dst_ref=table.at[pl.ds(pl.multiple_of(f * LEV + rows_of * SUB, SUB), SUB)],
            send_sem=field_send.at[i, f], recv_sem=field_recv.at[i, f],
            device_id=(to, tile), device_id_type=pl.DeviceIdType.MESH)

    def record_copies(i, to, slot):
        return [pltpu.make_async_remote_copy(
            src_ref=send_f.at[pl.ds(pl.multiple_of(to * ROWS, 8), ROWS)], dst_ref=recv_f.at[slot],
            send_sem=f_send.at[i], recv_sem=f_recv.at[i],
            device_id=(band, to), device_id_type=pl.DeviceIdType.MESH),
            pltpu.make_async_remote_copy(
            src_ref=send_c.at[to], dst_ref=recv_c.at[slot],
            send_sem=c_send.at[i], recv_sem=c_recv.at[i],
            device_id=(band, to), device_id_type=pl.DeviceIdType.MESH)]

    def send_fields(i, _):
        to = (band + i) % N_BAND
        for f in range(4):
            field_copy(i, f, to, band).start()
        return 0

    def send_records(i, _):
        for copy in record_copies(i, place(tile, i, 1), tile):
            copy.start()
        return 0

    lax.fori_loop(1, N_BAND, send_fields, 0)
    lax.fori_loop(1, N_TILE, send_records, 0)
    recv_f[tile] = send_f[pl.ds(pl.multiple_of(tile * ROWS, 8), ROWS), :]
    recv_c[tile] = send_c[tile]
    binned[...] = jnp.zeros_like(binned)
    for copy in own:
        copy.wait()

    def take_fields(i, _):
        source = (band + N_BAND - i) % N_BAND
        for f in range(4):
            field_copy(i, f, (band + i) % N_BAND, source).wait_recv()
        return 0

    lax.fori_loop(1, N_BAND, take_fields, 0)
    first = jnp.where(lax.broadcasted_iota(jnp.int32, (8, COLS), 1) == 0, 1.0, 0.0).astype(BF)
    east_out[...] = lax.dot_general(first, table[...], (((1,), (1,)), ((), ())), preferred_element_type=F32)
    west = (tile + N_TILE - 1) % N_TILE
    east_copy = pltpu.make_async_remote_copy(
        src_ref=east_out, dst_ref=east_in, send_sem=east_sems.at[0], recv_sem=east_sems.at[1],
        device_id=(band, west), device_id_type=pl.DeviceIdType.MESH)
    east_copy.start()
    split_levels(table, tperm)
    set_kappa(table, upper, lower)
    east_copy.wait()

    def body(i, carry):
        source = place(tile, i, -1)

        @pl.when(i > 0)
        def _():
            for copy in record_copies(i, place(tile, i, 1), source):
                copy.wait_recv()

        carry, ends = pivots(i, carry[0], upper, lower, inv)
        fr = recv_f[source, pl.ds(0, CAP, stride=4), :]
        h = recv_f[source, pl.ds(1, CAP, stride=4), :]
        n = recv_f[source, pl.ds(2, CAP, stride=4), :]
        m = recv_f[source, pl.ds(3, CAP, stride=4), :]
        col = recv_c[source].astype(F32)[:CAP]
        interpolate(fr, h, col, tperm, val)
        east = [east_in[:, f * LEV:(f + 1) * LEV] for f in range(4)]
        moved, low, a, b = move(fr, h, n, m, col, [val[f, 0:CAP, :] for f in range(4)], east)
        moved_ref[source] = moved
        binned[...] += binning(low, a, b, col)
        return carry, ends

    one = jnp.ones((1, COLS), F32)
    _, ends = lax.fori_loop(0, N_TILE, body, ((one, one), (one, one)))
    solve(ends, binned[...].T, upper, lower, inv, rhs, fwd, back, conc_ref)

    def sent_fields(i, _):
        for f in range(4):
            field_copy(i, f, (band + i) % N_BAND, band).wait_send()
        return 0

    def sent_records(i, _):
        for copy in record_copies(i, place(tile, i, 1), tile):
            copy.wait_send()
        return 0

    lax.fori_loop(1, N_BAND, sent_fields, 0)
    lax.fori_loop(1, N_TILE, sent_records, 0)


def shards(wind, temp, diff, removal, frac, height, mass, noise, column, dest):
    vm = pl.BlockSpec(memory_space=pltpu.VMEM)
    hbm = pl.BlockSpec(memory_space=pl.ANY)
    grid = pltpu.VMEM((LEV, COLS), F32)
    dma = pltpu.SemaphoreType.DMA
    conc, moved = pl.pallas_call(
        kernel,
        out_shape=(jax.ShapeDtypeStruct((LEV, COLS), F32), jax.ShapeDtypeStruct((N_TILE, CAP, PB), F32)),
        in_specs=[hbm] * 4 + [vm] * 6,
        out_specs=(vm, vm),
        scratch_shapes=[
            pltpu.VMEM((4 * LEV, COLS), BF), pltpu.VMEM((4 * LEV, COLS), BF),
            pltpu.VMEM((8, 4 * LEV), F32), pltpu.VMEM((8, 4 * LEV), F32),
            pltpu.VMEM((N_TILE * ROWS, PB), F32), pltpu.VMEM((N_TILE, 16, PB), BF),
            pltpu.VMEM((N_TILE, ROWS, PB), F32), pltpu.VMEM((N_TILE, 16, PB), BF),
            pltpu.VMEM((4, 16, PB), F32), pltpu.VMEM((COLS, LEV), F32),
            grid, grid, grid, grid, grid, grid,
            dma((N_BAND, 4)), dma((N_BAND, 4)), dma((4,)), dma((2,)),
            dma((N_TILE,)), dma((N_TILE,)), dma((N_TILE,)), dma((N_TILE,)),
        ],
        compiler_params=pltpu.CompilerParams(
            collective_id=0, has_side_effects=True, vmem_limit_bytes=48 * 2**20),
        cost_estimate=pl.CostEstimate(flops=2 * 40960 * 256 * 640, bytes_accessed=2 * 2**20, transcendentals=0),
    )(wind, temp, diff, removal, frac, height, noise, mass, column, dest.reshape(1, B_DEV))
    return conc[None], moved.reshape(N_TILE * CAP, PB)


def solution(mesh):
    read = P(None, "band", "tile")
    rec = P(("band", "tile"), None)
    return jax.shard_map(
        shards, mesh=mesh,
        in_specs=(read,) * 4 + (rec,) * 5 + (P(("band", "tile")),),
        out_specs=(P("band", None, "tile"), rec), check_vma=False)
```

```python
import jax
import jax.numpy as jnp
from jax import lax
from jax.experimental import pallas as pl
from jax.experimental.pallas import tpu as pltpu
from jax.sharding import PartitionSpec as P

LEV = 128
COLS = 256
CAP = 10
PB = 128
BIN = 8
CH = 2
F32 = jnp.float32
BF = jnp.bfloat16


def iota(shape, dim, dtype=F32):
    return lax.broadcasted_iota(jnp.int32, shape, dim).astype(dtype)


def split_levels(table_ref, tperm_ref):
    row = lax.broadcasted_iota(jnp.int32, (LEV, LEV), 0)
    col = lax.broadcasted_iota(jnp.int32, (LEV, LEV), 1)
    source = jnp.where(row < LEV // 2, 2 * row, 2 * row - (LEV - 1))
    perm = (col == source).astype(F32).astype(BF)
    for f in range(4):
        part = pl.ds(f * LEV, LEV)
        tperm_ref[part, :] = jnp.dot(perm, table_ref[part, :], preferred_element_type=F32).astype(BF)


def set_kappa(table_ref, upper_ref, lower_ref):
    k = table_ref[pl.ds(2 * LEV, LEV), :].astype(F32)
    kappa = 0.5 * (k[:-1] + k[1:])
    zero = jnp.zeros((1, COLS), F32)
    upper_ref[...] = jnp.concatenate([kappa, zero], axis=0)
    lower_ref[...] = jnp.concatenate([zero, kappa], axis=0)


def pivots(step, carry, upper_ref, lower_ref, inv_ref):
    top, bot = carry
    for i in range(LEV // 2 // NG):
        k = LEV // 2 // NG * step + i
        u = upper_ref[pl.ds(k, 1), :]
        inv = 1.0 / (top + u)
        inv_ref[pl.ds(k, 1), :] = inv
        last_top = top
        top = 1.0 + u * (top * inv)
        m = LEV - 1 - k
        low = lower_ref[pl.ds(m, 1), :]
        inv = 1.0 / (bot + low)
        inv_ref[pl.ds(m, 1), :] = inv
        last_bot = bot
        bot = 1.0 + low * (bot * inv)
    return (top, bot), (last_top, last_bot)


G = 4
NG = 8
R = G * CAP


def spread(x, c, rows, dtype=F32):
    return jnp.broadcast_to(x[c:c + 1], (rows, PB)).astype(dtype)


def move(fr, height, noise, mass, col, val, east):
    low = jnp.clip(jnp.floor(height), 0.0, LEV - 2.0)
    fz = height - low
    right = fr.astype(BF).astype(F32)
    edge = jnp.where(col == COLS - 1.0, right, 0.0)
    low_i = low.astype(jnp.int32)

    def picked(table, index):
        return jnp.concatenate([jnp.take_along_axis(table, index[r:r + 8], axis=1) for r in range(0, R, 8)], axis=0)

    w, temp, kd, rate = [
        val[f] + edge * (picked(east[f], low_i) * (1.0 - fz) + picked(east[f], low_i + 1) * fz) for f in range(4)]
    znew = jnp.clip(height + w + jnp.sqrt(2.0 * kd) * noise, 0.0, LEV - 1.0)
    moved = jnp.where(mass > 0, znew, 0.0)
    load = mass * jnp.exp(-rate) * temp
    low = jnp.clip(jnp.floor(znew), 0.0, LEV - 2.0)
    fz = znew - low
    return moved, low, load * (1.0 - fz), load * fz


def load_rows(low, load_lo, load_hi, c):
    lev = iota((LEV, PB), 0, BF)
    a = spread(load_lo, c, LEV, BF)
    b = spread(load_hi, c, LEV, BF)
    rest = jnp.where(lev == spread(low + 1.0, c, LEV, BF), b, jnp.zeros_like(b))
    return jnp.where(lev == spread(low, c, LEV, BF), a, rest)


def pick_rows(col, c):
    one = jnp.ones((COLS, PB), BF)
    return jnp.where(iota((COLS, PB), 0, BF) == spread(col, c, COLS, BF), one, jnp.zeros_like(one))


def bin_part(low, load_lo, load_hi, col, rows):
    picks = jnp.concatenate([pick_rows(col, c) for c in rows], axis=1)
    loads = jnp.concatenate([load_rows(low, load_lo, load_hi, c) for c in rows], axis=1)
    return lax.dot_general(picks, loads, (((1,), (1,)), ((), ())), preferred_element_type=F32)


def group_work(now, before, tperm_ref, val_ref, east):
    fr, height, col = now
    if before is not None:
        moved, b_low, b_lo, b_hi = move(*before, east)
        b_col = before[4]
    left = 1.0 - fr
    low = jnp.clip(jnp.floor(height), 0.0, LEV - 2.0)
    odd_i = jnp.floor(low * 0.5)
    even_i = jnp.floor((low + 1.0) * 0.5)
    w_even = jnp.maximum(0.0, 1.0 - jnp.abs(height - 2.0 * even_i))
    w_odd = jnp.maximum(0.0, 1.0 - jnp.abs(height - (2.0 * odd_i + 1.0)))
    g_even = jnp.floor(even_i * 0.125)
    g_odd = jnp.floor(odd_i * 0.125)
    s_even = even_i - 8.0 * g_even
    s_odd = odd_i - 8.0 * g_odd
    col1 = col + 1.0
    ids = iota((COLS, PB), 0, BF)
    sub = iota((8, PB), 0)
    zero = jnp.zeros((COLS, PB), BF)
    bins = None
    for c0 in range(0, R, CH):
        weights = []
        for c in range(c0, c0 + CH):
            rest = jnp.where(ids == spread(col1, c, COLS, BF), spread(fr, c, COLS, BF), zero)
            weights.append(jnp.where(ids == spread(col, c, COLS, BF), spread(left, c, COLS, BF), rest))
        horiz = jnp.dot(tperm_ref[...], jnp.concatenate(weights, axis=1), preferred_element_type=F32)
        for i in range(CH):
            c = c0 + i
            ge = spread(g_even, c, 8)
            go = spread(g_odd, c, 8)
            we = jnp.where(sub == spread(s_even, c, 8), spread(w_even, c, 8), 0.0)
            wo = jnp.where(sub == spread(s_odd, c, 8), spread(w_odd, c, 8), 0.0)
            e_masks = [ge >= float(g) for g in range(1, 8)]
            o_masks = [go >= float(g) for g in range(1, 8)]
            lanes = slice(i * PB, (i + 1) * PB)
            for f in range(4):
                base = f * LEV
                e = horiz[base:base + 8, lanes]
                o = horiz[base + 64:base + 72, lanes]
                for g in range(1, 8):
                    e = jnp.where(e_masks[g - 1], horiz[base + 8 * g:base + 8 * g + 8, lanes], e)
                    o = jnp.where(o_masks[g - 1], horiz[base + 64 + 8 * g:base + 72 + 8 * g, lanes], o)
                val_ref[f, c:c + 1, :] = jnp.sum(e * we + o * wo, axis=0, keepdims=True)
        if before is not None and (c0 + CH) % BIN == 0:
            part = bin_part(b_low, b_lo, b_hi, b_col, range(c0 + CH - BIN, c0 + CH))
            bins = part if bins is None else bins + part
    if before is not None:
        return moved, bins


def last_group(before, east):
    moved, low, lo, hi = move(*before, east)
    return moved, bin_part(low, lo, hi, before[4], range(R))


def solve(ends, binned, upper_ref, lower_ref, inv_ref, rhs_ref, fwd_ref, back_ref, out_ref):
    top, bot = ends
    half = LEV // 2
    inv = inv_ref[...]
    u, low = upper_ref[...], lower_ref[...]
    upper_rows = lax.broadcasted_iota(jnp.int32, (LEV, COLS), 0) < half
    rhs_ref[...] = binned * inv
    fwd_ref[...] = jnp.where(upper_rows, low, u) * inv
    back_ref[...] = jnp.where(upper_rows, u, low) * inv
    d = rhs_ref[0:1, :]
    e = rhs_ref[LEV - 1:LEV, :]
    ds, es = [d], [e]
    for k in range(1, half):
        m = LEV - 1 - k
        d = rhs_ref[k:k + 1, :] + fwd_ref[k:k + 1, :] * d
        e = rhs_ref[m:m + 1, :] + fwd_ref[m:m + 1, :] * e
        ds.append(d)
        es.append(e)
    kappa = upper_ref[half - 1:half, :]
    alpha = back_ref[half - 1:half, :]
    beta = back_ref[half:half + 1, :]
    det = (kappa * (top + bot) + top * bot) * inv_ref[half - 1:half, :] * inv_ref[half:half + 1, :]
    x = (d + alpha * e) / det
    y = e + beta * x
    out_ref[half - 1:half, :] = x
    out_ref[half:half + 1, :] = y
    for k in range(half - 2, -1, -1):
        m = LEV - 1 - k
        x = ds[k] + back_ref[k:k + 1, :] * x
        y = es[k] + back_ref[m:m + 1, :] * y
        out_ref[k:k + 1, :] = x
        out_ref[m:m + 1, :] = y


N_BAND = 8
N_TILE = 32
NY, NZ = 4, 8
B_DEV = 160
SUB = LEV // N_BAND
ROWS = 4 * CAP


def offset(i):
    q, dy = i // NY, i % NY
    dz = ((q + 1) // 2) * (q % 2) + ((NZ - q // 2) % NZ) * (1 - q % 2)
    return dy, dz


def place(tile, i, sign):
    dy, dz = offset(i)
    y = (tile // NZ + NY + sign * dy) % NY
    z = (tile % NZ + NZ + sign * dz) % NZ
    return y * NZ + z


def build(dest_ref, parts, col_ref, send_f, send_c):
    dest = dest_ref[...].astype(F32)
    wide = jnp.broadcast_to(dest, (B_DEV, B_DEV))
    row = lax.broadcasted_iota(jnp.int32, (B_DEV, B_DEV), 0)
    lane = lax.broadcasted_iota(jnp.int32, (B_DEV, B_DEV), 1)
    tall = jnp.sum(jnp.where(row == lane, wide, 0.0), axis=1, keepdims=True)
    same = jnp.where((tall == wide) & (row < lane), 1.0, 0.0)
    rank = jnp.sum(same, axis=0, keepdims=True)
    slots = N_TILE * CAP
    pick = jnp.where(iota((slots, B_DEV), 0) == dest * CAP + rank, 1.0, 0.0).astype(BF)
    for f, ref in enumerate(parts):
        x = ref[...]
        hi = x.astype(BF)
        rest = x - hi.astype(F32)
        mid = rest.astype(BF)
        low = (rest - mid.astype(F32)).astype(BF)
        total = jnp.dot(pick, hi, preferred_element_type=F32)
        total = total + jnp.dot(pick, mid, preferred_element_type=F32)
        total = total + jnp.dot(pick, low, preferred_element_type=F32)
        send_f[pl.ds(f, slots, stride=4), :] = total
    pick = jnp.where(iota((N_TILE * 16, B_DEV), 0) == dest * 16 + rank, 1.0, 0.0).astype(BF)
    cols = jnp.dot(pick, col_ref[...].astype(F32).astype(BF), preferred_element_type=F32)
    send_c[...] = cols.astype(BF).reshape(N_TILE, 16, PB)


def kernel(wind, temp, diff, removal, frac, height, noise, mass, column, dest,
           conc_ref, moved_ref,
           table, tperm, east_out, east_in, send_f, send_c, recv_f, recv_c,
           in_f, in_c, in_d, val, val_old, binned, upper, lower, inv, rhs, fwd, back,
           field_send, field_recv, own_sem, in_sem, east_sems, f_send, f_recv, c_send, c_recv):
    band, tile = lax.axis_index("band"), lax.axis_index("tile")
    barrier = pltpu.get_barrier_semaphore()

    def greet_tile(i, _):
        pl.semaphore_signal(barrier, inc=1, device_id=(band, place(tile, i, 1)), device_id_type=pl.DeviceIdType.MESH)
        return 0

    def greet_band(i, _):
        pl.semaphore_signal(barrier, inc=1, device_id=((band + i) % N_BAND, tile), device_id_type=pl.DeviceIdType.MESH)
        return 0

    loads = [pltpu.make_async_copy(ref, in_f.at[f], in_sem.at[f]) for f, ref in enumerate((frac, height, noise, mass))]
    loads.append(pltpu.make_async_copy(column, in_c, in_sem.at[4]))
    loads.append(pltpu.make_async_copy(dest, in_d, in_sem.at[5]))
    for copy in loads:
        copy.start()
    lax.fori_loop(1, N_TILE, greet_tile, 0)
    lax.fori_loop(1, N_BAND, greet_band, 0)
    fields = (wind, temp, diff, removal)
    own = [pltpu.make_async_copy(ref.at[band], table.at[pl.ds(pl.multiple_of(f * LEV + band * SUB, SUB), SUB)], own_sem.at[f])
           for f, ref in enumerate(fields)]
    for copy in own:
        copy.start()
    for copy in loads:
        copy.wait()
    build(in_d, [in_f.at[f] for f in range(4)], in_c, send_f, send_c)
    pl.semaphore_wait(barrier, N_TILE + N_BAND - 2)

    def field_copy(i, f, to, rows_of):
        return pltpu.make_async_remote_copy(
            src_ref=fields[f].at[to], dst_ref=table.at[pl.ds(pl.multiple_of(f * LEV + rows_of * SUB, SUB), SUB)],
            send_sem=field_send.at[i, f], recv_sem=field_recv.at[i, f],
            device_id=(to, tile), device_id_type=pl.DeviceIdType.MESH)

    def record_copies(i):
        to = place(tile, i, 1)
        return [pltpu.make_async_remote_copy(
            src_ref=send_f.at[pl.ds(pl.multiple_of(to * ROWS, 8), ROWS)], dst_ref=recv_f.at[i // G, pl.ds(pl.multiple_of(i % G * ROWS, 8), ROWS)],
            send_sem=f_send.at[i], recv_sem=f_recv.at[i],
            device_id=(band, to), device_id_type=pl.DeviceIdType.MESH),
            pltpu.make_async_remote_copy(
            src_ref=send_c.at[to], dst_ref=recv_c.at[i],
            send_sem=c_send.at[i], recv_sem=c_recv.at[i],
            device_id=(band, to), device_id_type=pl.DeviceIdType.MESH)]

    def send_fields(i, _):
        to = (band + i) % N_BAND
        for f in range(4):
            field_copy(i, f, to, band).start()
        return 0

    def send_records(i, _):
        for copy in record_copies(i):
            copy.start()
        return 0

    lax.fori_loop(1, N_BAND, send_fields, 0)
    lax.fori_loop(1, N_TILE, send_records, 0)
    recv_f[0, 0:ROWS, :] = send_f[pl.ds(pl.multiple_of(tile * ROWS, 8), ROWS), :]
    recv_c[0] = send_c[tile]
    binned[...] = jnp.zeros_like(binned)
    for copy in own:
        copy.wait()

    def take_fields(i, _):
        source = (band + N_BAND - i) % N_BAND
        for f in range(4):
            field_copy(i, f, (band + i) % N_BAND, source).wait_recv()
        return 0

    lax.fori_loop(1, N_BAND, take_fields, 0)
    first = jnp.where(lax.broadcasted_iota(jnp.int32, (8, COLS), 1) == 0, 1.0, 0.0).astype(BF)
    east_out[...] = lax.dot_general(first, table[...], (((1,), (1,)), ((), ())), preferred_element_type=F32)
    west = (tile + N_TILE - 1) % N_TILE
    east_copy = pltpu.make_async_remote_copy(
        src_ref=east_out, dst_ref=east_in, send_sem=east_sems.at[0], recv_sem=east_sems.at[1],
        device_id=(band, west), device_id_type=pl.DeviceIdType.MESH)
    east_copy.start()
    split_levels(table, tperm)
    set_kappa(table, upper, lower)
    def take_records(i, _):
        for copy in record_copies(i):
            copy.wait_recv()
        return 0

    def rows_of(q):
        return [recv_f[q, pl.ds(f, R, stride=4), :] for f in range(4)]

    def col_of(q):
        return jnp.concatenate([recv_c[q * G + j].astype(F32)[:CAP] for j in range(G)], axis=0)

    def before_of(q):
        return (*rows_of(q), col_of(q), [val_old[f] for f in range(4)])

    def put(q, moved):
        for j in range(G):
            moved_ref[place(tile, q * G + j, -1)] = moved[j * CAP:(j + 1) * CAP]

    lax.fori_loop(1, G, take_records, 0)
    one = jnp.ones((1, COLS), F32)
    carry = pivots(0, (one, one), upper, lower, inv)
    fr, h, _, _ = rows_of(0)
    group_work((fr, h, col_of(0)), None, tperm, val_old, None)
    east_copy.wait()
    east = [east_in[:, f * LEV:(f + 1) * LEV] for f in range(4)]

    def body(q, carry):
        lax.fori_loop(q * G, q * G + G, take_records, 0)
        carry, ends = pivots(q, carry[0], upper, lower, inv)
        fr, h, _, _ = rows_of(q)
        moved, bins = group_work((fr, h, col_of(q)), before_of(q - 1), tperm, val, east)
        put(q - 1, moved)
        binned[...] += bins
        val_old[...] = val[...]
        return carry, ends

    _, ends = lax.fori_loop(1, NG, body, carry)
    moved, bins = last_group(before_of(NG - 1), east)
    put(NG - 1, moved)
    solve(ends, (binned[...] + bins).T, upper, lower, inv, rhs, fwd, back, conc_ref)

    def sent_fields(i, _):
        for f in range(4):
            field_copy(i, f, (band + i) % N_BAND, band).wait_send()
        return 0

    def sent_records(i, _):
        for copy in record_copies(i):
            copy.wait_send()
        return 0

    lax.fori_loop(1, N_BAND, sent_fields, 0)
    lax.fori_loop(1, N_TILE, sent_records, 0)


def shards(wind, temp, diff, removal, frac, height, mass, noise, column, dest):
    vm = pl.BlockSpec(memory_space=pltpu.VMEM)
    hbm = pl.BlockSpec(memory_space=pltpu.HBM)
    grid = pltpu.VMEM((LEV, COLS), F32)
    dma = pltpu.SemaphoreType.DMA
    conc, moved = pl.pallas_call(
        kernel,
        out_shape=(jax.ShapeDtypeStruct((LEV, COLS), F32), jax.ShapeDtypeStruct((N_TILE, CAP, PB), F32)),
        in_specs=[hbm] * 10,
        out_specs=(vm, vm),
        scratch_shapes=[
            pltpu.VMEM((4 * LEV, COLS), BF), pltpu.VMEM((4 * LEV, COLS), BF),
            pltpu.VMEM((8, 4 * LEV), F32), pltpu.VMEM((8, 4 * LEV), F32),
            pltpu.VMEM((N_TILE * ROWS, PB), F32), pltpu.VMEM((N_TILE, 16, PB), BF),
            pltpu.VMEM((NG, G * ROWS, PB), F32), pltpu.VMEM((N_TILE, 16, PB), BF),
            pltpu.VMEM((4, B_DEV, PB), F32), pltpu.VMEM((B_DEV, PB), jnp.int32), pltpu.VMEM((1, B_DEV), jnp.int32),
            pltpu.VMEM((4, R, PB), F32), pltpu.VMEM((4, R, PB), F32), pltpu.VMEM((COLS, LEV), F32),
            grid, grid, grid, grid, grid, grid,
            dma((N_BAND, 4)), dma((N_BAND, 4)), dma((4,)), dma((6,)), dma((2,)),
            dma((N_TILE,)), dma((N_TILE,)), dma((N_TILE,)), dma((N_TILE,)),
        ],
        compiler_params=pltpu.CompilerParams(
            collective_id=0, has_side_effects=True, vmem_limit_bytes=63 * 2**20),
        cost_estimate=pl.CostEstimate(flops=2 * 40960 * 256 * 640, bytes_accessed=2 * 2**20, transcendentals=0),
    )(wind, temp, diff, removal, frac, height, noise, mass, column, dest.reshape(1, B_DEV))
    return conc[None], moved.reshape(N_TILE * CAP, PB)


def solution(mesh):
    read = P(None, "band", "tile")
    rec = P(("band", "tile"), None)
    return jax.shard_map(
        shards, mesh=mesh,
        in_specs=(read,) * 4 + (rec,) * 5 + (P(("band", "tile")),),
        out_specs=(P("band", None, "tile"), rec), check_vma=False)
```

```python
import jax
import jax.numpy as jnp
from jax import lax
from jax.experimental import pallas as pl
from jax.experimental.pallas import tpu as pltpu
from jax.sharding import PartitionSpec as P

LEV = 128
COLS = 256
CAP = 10
PB = 128
CH = 2
F32 = jnp.float32
BF = jnp.bfloat16


def iota(shape, dim, dtype=F32):
    return lax.broadcasted_iota(jnp.int32, shape, dim).astype(dtype)


def split_levels(table_ref, tperm_ref):
    row = lax.broadcasted_iota(jnp.int32, (LEV, LEV), 0)
    col = lax.broadcasted_iota(jnp.int32, (LEV, LEV), 1)
    source = jnp.where(row < LEV // 2, 2 * row, 2 * row - (LEV - 1))
    perm = (col == source).astype(F32).astype(BF)
    for f in range(4):
        part = pl.ds(f * LEV, LEV)
        tperm_ref[part, :] = jnp.dot(perm, table_ref[part, :], preferred_element_type=F32).astype(BF)


def set_kappa(table_ref, upper_ref, lower_ref):
    k = table_ref[pl.ds(2 * LEV, LEV), :].astype(F32)
    kappa = 0.5 * (k[:-1] + k[1:])
    zero = jnp.zeros((1, COLS), F32)
    upper_ref[...] = jnp.concatenate([kappa, zero], axis=0)
    lower_ref[...] = jnp.concatenate([zero, kappa], axis=0)


def pivots(step, carry, upper_ref, lower_ref, inv_ref):
    top, bot = carry
    for i in range(LEV // 2 // NG):
        k = LEV // 2 // NG * step + i
        u = upper_ref[pl.ds(k, 1), :]
        inv = 1.0 / (top + u)
        inv_ref[pl.ds(k, 1), :] = inv
        last_top = top
        top = 1.0 + u * (top * inv)
        m = LEV - 1 - k
        low = lower_ref[pl.ds(m, 1), :]
        inv = 1.0 / (bot + low)
        inv_ref[pl.ds(m, 1), :] = inv
        last_bot = bot
        bot = 1.0 + low * (bot * inv)
    return (top, bot), (last_top, last_bot)


G = 4
NG = 8
R = G * CAP


def spread(x, c, rows, dtype=F32):
    return jnp.broadcast_to(x[c:c + 1], (rows, PB)).astype(dtype)


def move(fr, height, noise, mass, col, val, east):
    low = jnp.clip(jnp.floor(height), 0.0, LEV - 2.0)
    fz = height - low
    right = fr.astype(BF).astype(F32)
    edge = jnp.where(col == COLS - 1.0, right, 0.0)
    low_i = low.astype(jnp.int32)

    def picked(table, index):
        return jnp.concatenate([jnp.take_along_axis(table, index[r:r + 8], axis=1) for r in range(0, R, 8)], axis=0)

    w, temp, kd, rate = [
        val[f] + edge * (picked(east[f], low_i) * (1.0 - fz) + picked(east[f], low_i + 1) * fz) for f in range(4)]
    znew = jnp.clip(height + w + jnp.sqrt(2.0 * kd) * noise, 0.0, LEV - 1.0)
    moved = jnp.where(mass > 0, znew, 0.0)
    load = mass * jnp.exp(-rate) * temp
    low = jnp.clip(jnp.floor(znew), 0.0, LEV - 2.0)
    fz = znew - low
    return moved, low, load * (1.0 - fz), load * fz


def load_rows(low, load_lo, load_hi, c):
    lev = iota((LEV, PB), 0, BF)
    a = spread(load_lo, c, LEV, BF)
    b = spread(load_hi, c, LEV, BF)
    rest = jnp.where(lev == spread(low + 1.0, c, LEV, BF), b, jnp.zeros_like(b))
    return jnp.where(lev == spread(low, c, LEV, BF), a, rest)


def bin_rows(low, load_lo, load_hi, col):
    loads = jnp.concatenate([load_rows(low, load_lo, load_hi, c) for c in range(R)], axis=1)
    turned = jnp.concatenate([col, jnp.zeros((PB - R, PB), F32)], axis=0).T.astype(BF)
    lanes = iota((PB, COLS), 1, BF)
    one = jnp.ones((PB, COLS), BF)
    picks = jnp.concatenate(
        [jnp.where(lanes == jnp.broadcast_to(turned[:, c:c + 1], (PB, COLS)), one, jnp.zeros_like(one)) for c in range(R)],
        axis=0)
    return jnp.dot(loads, picks, preferred_element_type=F32)


def group_work(now, before, tperm_ref, val_ref, east):
    fr, height, col = now
    if before is not None:
        moved, b_low, b_lo, b_hi = move(*before, east)
    left = 1.0 - fr
    low = jnp.clip(jnp.floor(height), 0.0, LEV - 2.0)
    odd_i = jnp.floor(low * 0.5)
    even_i = jnp.floor((low + 1.0) * 0.5)
    w_even = jnp.maximum(0.0, 1.0 - jnp.abs(height - 2.0 * even_i))
    w_odd = jnp.maximum(0.0, 1.0 - jnp.abs(height - (2.0 * odd_i + 1.0)))
    g_even = jnp.floor(even_i * 0.125)
    g_odd = jnp.floor(odd_i * 0.125)
    s_even = even_i - 8.0 * g_even
    s_odd = odd_i - 8.0 * g_odd
    col1 = col + 1.0
    ids = iota((COLS, PB), 0, BF)
    sub = iota((8, PB), 0)
    zero = jnp.zeros((COLS, PB), BF)
    for c0 in range(0, R, CH):
        weights = []
        for c in range(c0, c0 + CH):
            rest = jnp.where(ids == spread(col1, c, COLS, BF), spread(fr, c, COLS, BF), zero)
            weights.append(jnp.where(ids == spread(col, c, COLS, BF), spread(left, c, COLS, BF), rest))
        horiz = jnp.dot(tperm_ref[...], jnp.concatenate(weights, axis=1), preferred_element_type=F32)
        for i in range(CH):
            c = c0 + i
            ge = spread(g_even, c, 8)
            go = spread(g_odd, c, 8)
            we = jnp.where(sub == spread(s_even, c, 8), spread(w_even, c, 8), 0.0)
            wo = jnp.where(sub == spread(s_odd, c, 8), spread(w_odd, c, 8), 0.0)
            e_masks = [ge >= float(g) for g in range(1, 8)]
            o_masks = [go >= float(g) for g in range(1, 8)]
            lanes = slice(i * PB, (i + 1) * PB)
            for f in range(4):
                base = f * LEV
                e = horiz[base:base + 8, lanes]
                o = horiz[base + 64:base + 72, lanes]
                for g in range(1, 8):
                    e = jnp.where(e_masks[g - 1], horiz[base + 8 * g:base + 8 * g + 8, lanes], e)
                    o = jnp.where(o_masks[g - 1], horiz[base + 64 + 8 * g:base + 72 + 8 * g, lanes], o)
                val_ref[f, c:c + 1, :] = jnp.sum(e * we + o * wo, axis=0, keepdims=True)
    if before is not None:
        return moved, bin_rows(b_low, b_lo, b_hi, before[4])


def last_group(before, east):
    moved, low, lo, hi = move(*before, east)
    return moved, bin_rows(low, lo, hi, before[4])


def solve(ends, binned, upper_ref, lower_ref, inv_ref, rhs_ref, fwd_ref, back_ref, out_ref):
    top, bot = ends
    half = LEV // 2
    inv = inv_ref[...]
    u, low = upper_ref[...], lower_ref[...]
    upper_rows = lax.broadcasted_iota(jnp.int32, (LEV, COLS), 0) < half
    rhs_ref[...] = binned * inv
    fwd_ref[...] = jnp.where(upper_rows, low, u) * inv
    back_ref[...] = jnp.where(upper_rows, u, low) * inv
    d = rhs_ref[0:1, :]
    e = rhs_ref[LEV - 1:LEV, :]
    ds, es = [d], [e]
    for k in range(1, half):
        m = LEV - 1 - k
        d = rhs_ref[k:k + 1, :] + fwd_ref[k:k + 1, :] * d
        e = rhs_ref[m:m + 1, :] + fwd_ref[m:m + 1, :] * e
        ds.append(d)
        es.append(e)
    kappa = upper_ref[half - 1:half, :]
    alpha = back_ref[half - 1:half, :]
    beta = back_ref[half:half + 1, :]
    det = (kappa * (top + bot) + top * bot) * inv_ref[half - 1:half, :] * inv_ref[half:half + 1, :]
    x = (d + alpha * e) / det
    y = e + beta * x
    out_ref[half - 1:half, :] = x
    out_ref[half:half + 1, :] = y
    for k in range(half - 2, -1, -1):
        m = LEV - 1 - k
        x = ds[k] + back_ref[k:k + 1, :] * x
        y = es[k] + back_ref[m:m + 1, :] * y
        out_ref[k:k + 1, :] = x
        out_ref[m:m + 1, :] = y


N_BAND = 8
N_TILE = 32
NY, NZ = 4, 8
B_DEV = 160
AHEAD = 5
SUB = LEV // N_BAND
ROWS = 4 * CAP


def offset(i):
    j = (i + NY) // (2 * NY)
    r = (i + NY) % (2 * NY)
    dy = (1 - (j + 7) // 8) * (r % NY) + ((j + 7) // 8) * (r // 2)
    dz = (j + (r % 2) * (NZ - 2 * j)) % NZ
    dz = dz * (1 - j // 4) + 4 * (j // 4)
    dy = dy * (1 - j // 4) + (j // 4) * (r % NY)
    return dy, dz


def place(tile, i, sign):
    dy, dz = offset(i)
    y = (tile // NZ + NY + sign * dy) % NY
    z = (tile % NZ + NZ + sign * dz) % NZ
    return y * NZ + z


def build(dest_ref, parts, col_ref, send_f, send_c):
    dest = dest_ref[...].astype(F32)
    wide = jnp.broadcast_to(dest, (B_DEV, B_DEV))
    row = lax.broadcasted_iota(jnp.int32, (B_DEV, B_DEV), 0)
    lane = lax.broadcasted_iota(jnp.int32, (B_DEV, B_DEV), 1)
    tall = jnp.sum(jnp.where(row == lane, wide, 0.0), axis=1, keepdims=True)
    same = jnp.where((tall == wide) & (row < lane), 1.0, 0.0)
    rank = jnp.sum(same, axis=0, keepdims=True)
    slots = N_TILE * CAP
    pick = jnp.where(iota((slots, B_DEV), 0) == dest * CAP + rank, 1.0, 0.0).astype(BF)
    for f, ref in enumerate(parts):
        x = ref[...]
        hi = x.astype(BF)
        rest = x - hi.astype(F32)
        mid = rest.astype(BF)
        low = (rest - mid.astype(F32)).astype(BF)
        total = jnp.dot(pick, hi, preferred_element_type=F32)
        total = total + jnp.dot(pick, mid, preferred_element_type=F32)
        total = total + jnp.dot(pick, low, preferred_element_type=F32)
        send_f[pl.ds(f, slots, stride=4), :] = total
    pick = jnp.where(iota((N_TILE * 16, B_DEV), 0) == dest * 16 + rank, 1.0, 0.0).astype(BF)
    cols = jnp.dot(pick, col_ref[...].astype(F32).astype(BF), preferred_element_type=F32)
    send_c[...] = cols.astype(BF).reshape(N_TILE, 16, PB)


def kernel(wind, temp, diff, removal, frac, height, noise, mass, column, dest,
           conc_ref, moved_ref,
           table, tperm, east_out, east_in, send_f, send_c, recv_f, recv_c,
           in_f, in_c, in_d, val, val_old, binned, upper, lower, inv, rhs, fwd, back,
           field_send, field_recv, own_sem, in_sem, east_sems, f_send, f_recv, c_send, c_recv):
    band, tile = lax.axis_index("band"), lax.axis_index("tile")
    barrier = pltpu.get_barrier_semaphore()

    def greet_tile(i, _):
        pl.semaphore_signal(barrier, inc=1, device_id=(band, place(tile, i, 1)), device_id_type=pl.DeviceIdType.MESH)
        return 0

    def greet_band(i, _):
        pl.semaphore_signal(barrier, inc=1, device_id=((band + i) % N_BAND, tile), device_id_type=pl.DeviceIdType.MESH)
        return 0

    loads = [pltpu.make_async_copy(ref, in_f.at[f], in_sem.at[f]) for f, ref in enumerate((frac, height, noise, mass))]
    loads.append(pltpu.make_async_copy(column, in_c, in_sem.at[4]))
    loads.append(pltpu.make_async_copy(dest, in_d, in_sem.at[5]))
    for copy in loads:
        copy.start()
    lax.fori_loop(1, N_TILE, greet_tile, 0)
    lax.fori_loop(1, N_BAND, greet_band, 0)
    fields = (wind, temp, diff, removal)
    own = [pltpu.make_async_copy(ref.at[band], table.at[pl.ds(pl.multiple_of(f * LEV + band * SUB, SUB), SUB)], own_sem.at[f])
           for f, ref in enumerate(fields)]
    for copy in own:
        copy.start()
    pl.semaphore_wait(barrier, N_TILE + N_BAND - 2)

    def field_copy(i, f, to, rows_of):
        return pltpu.make_async_remote_copy(
            src_ref=fields[f].at[to], dst_ref=table.at[pl.ds(pl.multiple_of(f * LEV + rows_of * SUB, SUB), SUB)],
            send_sem=field_send.at[i, f], recv_sem=field_recv.at[i, f],
            device_id=(to, tile), device_id_type=pl.DeviceIdType.MESH)

    def record_copies(i):
        to = place(tile, i, 1)
        return [pltpu.make_async_remote_copy(
            src_ref=send_f.at[pl.ds(pl.multiple_of(to * ROWS, 8), ROWS)], dst_ref=recv_f.at[i // G, pl.ds(pl.multiple_of(i % G * ROWS, 8), ROWS)],
            send_sem=f_send.at[i], recv_sem=f_recv.at[i],
            device_id=(band, to), device_id_type=pl.DeviceIdType.MESH),
            pltpu.make_async_remote_copy(
            src_ref=send_c.at[to], dst_ref=recv_c.at[i],
            send_sem=c_send.at[i], recv_sem=c_recv.at[i],
            device_id=(band, to), device_id_type=pl.DeviceIdType.MESH)]

    def send_fields(i, _):
        to = (band + i) % N_BAND
        for f in range(4):
            field_copy(i, f, to, band).start()
        return 0

    def send_records(i, _):
        for copy in record_copies(i):
            copy.start()
        return 0

    lax.fori_loop(1, N_BAND, send_fields, 0)
    for copy in loads:
        copy.wait()
    build(in_d, [in_f.at[f] for f in range(4)], in_c, send_f, send_c)
    lax.fori_loop(1, AHEAD * G, send_records, 0)
    recv_f[0, 0:ROWS, :] = send_f[pl.ds(pl.multiple_of(tile * ROWS, 8), ROWS), :]
    recv_c[0] = send_c[tile]
    binned[...] = jnp.zeros_like(binned)
    for copy in own:
        copy.wait()

    def take_fields(i, _):
        source = (band + N_BAND - i) % N_BAND
        for f in range(4):
            field_copy(i, f, (band + i) % N_BAND, source).wait_recv()
        return 0

    lax.fori_loop(1, N_BAND, take_fields, 0)
    first = jnp.where(lax.broadcasted_iota(jnp.int32, (8, COLS), 1) == 0, 1.0, 0.0).astype(BF)
    east_out[...] = lax.dot_general(first, table[...], (((1,), (1,)), ((), ())), preferred_element_type=F32)
    west = (tile + N_TILE - 1) % N_TILE
    east_copy = pltpu.make_async_remote_copy(
        src_ref=east_out, dst_ref=east_in, send_sem=east_sems.at[0], recv_sem=east_sems.at[1],
        device_id=(band, west), device_id_type=pl.DeviceIdType.MESH)
    east_copy.start()
    split_levels(table, tperm)
    set_kappa(table, upper, lower)
    def take_records(i, _):
        for copy in record_copies(i):
            copy.wait_recv()
        return 0

    def rows_of(q):
        return [recv_f[q, pl.ds(f, R, stride=4), :] for f in range(4)]

    def col_of(q):
        return jnp.concatenate([recv_c[q * G + j].astype(F32)[:CAP] for j in range(G)], axis=0)

    def before_of(q):
        return (*rows_of(q), col_of(q), [val_old[f] for f in range(4)])

    def put(q, moved):
        for j in range(G):
            moved_ref[pl.ds(place(tile, q * G + j, -1) * CAP, CAP), :] = moved[j * CAP:(j + 1) * CAP]

    lax.fori_loop(1, G, take_records, 0)
    one = jnp.ones((1, COLS), F32)
    carry = pivots(0, (one, one), upper, lower, inv)
    fr, h, _, _ = rows_of(0)
    group_work((fr, h, col_of(0)), None, tperm, val_old, None)
    east_copy.wait()
    east = [east_in[:, f * LEV:(f + 1) * LEV] for f in range(4)]

    def body(q, carry):
        lax.fori_loop(q * G, q * G + G, take_records, 0)
        first = jnp.minimum((q + AHEAD - 1) * G, N_TILE)
        lax.fori_loop(first, jnp.minimum(first + G, N_TILE), send_records, 0)
        carry, ends = pivots(q, carry[0], upper, lower, inv)
        fr, h, _, _ = rows_of(q)
        moved, bins = group_work((fr, h, col_of(q)), before_of(q - 1), tperm, val, east)
        put(q - 1, moved)
        binned[...] += bins
        val_old[...] = val[...]
        return carry, ends

    _, ends = lax.fori_loop(1, NG, body, carry)
    moved, bins = last_group(before_of(NG - 1), east)
    put(NG - 1, moved)
    solve(ends, binned[...] + bins, upper, lower, inv, rhs, fwd, back, conc_ref)

    def sent_fields(i, _):
        for f in range(4):
            field_copy(i, f, (band + i) % N_BAND, band).wait_send()
        return 0

    def sent_records(i, _):
        for copy in record_copies(i):
            copy.wait_send()
        return 0

    lax.fori_loop(1, N_BAND, sent_fields, 0)
    lax.fori_loop(1, N_TILE, sent_records, 0)


def shards(wind, temp, diff, removal, frac, height, mass, noise, column, dest):
    vm = pl.BlockSpec(memory_space=pltpu.VMEM)
    hbm = pl.BlockSpec(memory_space=pltpu.HBM)
    grid = pltpu.VMEM((LEV, COLS), F32)
    dma = pltpu.SemaphoreType.DMA
    conc, moved = pl.pallas_call(
        kernel,
        out_shape=(jax.ShapeDtypeStruct((LEV, COLS), F32), jax.ShapeDtypeStruct((N_TILE * CAP, PB), F32)),
        in_specs=[hbm] * 10,
        out_specs=(vm, vm),
        scratch_shapes=[
            pltpu.VMEM((4 * LEV, COLS), BF), pltpu.VMEM((4 * LEV, COLS), BF),
            pltpu.VMEM((8, 4 * LEV), F32), pltpu.VMEM((8, 4 * LEV), F32),
            pltpu.VMEM((N_TILE * ROWS, PB), F32), pltpu.VMEM((N_TILE, 16, PB), BF),
            pltpu.VMEM((NG, G * ROWS, PB), F32), pltpu.VMEM((N_TILE, 16, PB), BF),
            pltpu.VMEM((4, B_DEV, PB), F32), pltpu.VMEM((B_DEV, PB), jnp.int32), pltpu.VMEM((1, B_DEV), jnp.int32),
            pltpu.VMEM((4, R, PB), F32), pltpu.VMEM((4, R, PB), F32), grid,
            grid, grid, grid, grid, grid, grid,
            dma((N_BAND, 4)), dma((N_BAND, 4)), dma((4,)), dma((6,)), dma((2,)),
            dma((N_TILE,)), dma((N_TILE,)), dma((N_TILE,)), dma((N_TILE,)),
        ],
        compiler_params=pltpu.CompilerParams(
            collective_id=0, has_side_effects=True, vmem_limit_bytes=63 * 2**20),
        cost_estimate=pl.CostEstimate(flops=2 * 40960 * 256 * 640, bytes_accessed=2 * 2**20, transcendentals=0),
    )(wind, temp, diff, removal, frac, height, noise, mass, column, dest.reshape(1, B_DEV))
    return conc[None], moved


def solution(mesh):
    read = P(None, "band", "tile")
    rec = P(("band", "tile"), None)
    return jax.shard_map(
        shards, mesh=mesh,
        in_specs=(read,) * 4 + (rec,) * 5 + (P(("band", "tile")),),
        out_specs=(P("band", None, "tile"), rec), check_vma=False)
```

```python
import jax
import jax.numpy as jnp
from jax import lax
from jax.experimental import pallas as pl
from jax.experimental.pallas import tpu as pltpu
from jax.sharding import PartitionSpec as P

LEV = 128
COLS = 256
CAP = 10
PB = 128
CH = 2
F32 = jnp.float32
BF = jnp.bfloat16


def iota(shape, dim, dtype=F32):
    return lax.broadcasted_iota(jnp.int32, shape, dim).astype(dtype)


def split_levels(table_ref, tperm_ref):
    row = lax.broadcasted_iota(jnp.int32, (LEV, LEV), 0)
    col = lax.broadcasted_iota(jnp.int32, (LEV, LEV), 1)
    source = jnp.where(row < LEV // 2, 2 * row, 2 * row - (LEV - 1))
    perm = (col == source).astype(F32).astype(BF)
    for f in range(4):
        part = pl.ds(f * LEV, LEV)
        tperm_ref[part, :] = jnp.dot(perm, table_ref[part, :], preferred_element_type=F32).astype(BF)


def set_kappa(table_ref, upper_ref, lower_ref):
    k = table_ref[pl.ds(2 * LEV, LEV), :].astype(F32)
    kappa = 0.5 * (k[:-1] + k[1:])
    zero = jnp.zeros((1, COLS), F32)
    upper_ref[...] = jnp.concatenate([kappa, zero], axis=0)
    lower_ref[...] = jnp.concatenate([zero, kappa], axis=0)


def pivots(step, carry, upper_ref, lower_ref, inv_ref):
    top, bot = carry
    for i in range(LEV // 2 // NG):
        k = LEV // 2 // NG * step + i
        u = upper_ref[pl.ds(k, 1), :]
        inv = 1.0 / (top + u)
        inv_ref[pl.ds(k, 1), :] = inv
        last_top = top
        top = 1.0 + u * (top * inv)
        m = LEV - 1 - k
        low = lower_ref[pl.ds(m, 1), :]
        inv = 1.0 / (bot + low)
        inv_ref[pl.ds(m, 1), :] = inv
        last_bot = bot
        bot = 1.0 + low * (bot * inv)
    return (top, bot), (last_top, last_bot)


G = 4
NG = 8
R = G * CAP


def spread(x, c, rows, dtype=F32):
    return jnp.broadcast_to(x[c:c + 1], (rows, PB)).astype(dtype)


def move(fr, height, noise, mass, col, val, east):
    low = jnp.clip(jnp.floor(height), 0.0, LEV - 2.0)
    fz = height - low
    right = fr.astype(BF).astype(F32)
    edge = jnp.where(col == COLS - 1.0, right, 0.0)
    low_i = low.astype(jnp.int32)

    def picked(table, index):
        return jnp.concatenate([jnp.take_along_axis(table, index[r:r + 8], axis=1) for r in range(0, R, 8)], axis=0)

    w, temp, kd, rate = [
        val[f] + edge * (picked(east[f], low_i) * (1.0 - fz) + picked(east[f], low_i + 1) * fz) for f in range(4)]
    znew = jnp.clip(height + w + jnp.sqrt(2.0 * kd) * noise, 0.0, LEV - 1.0)
    moved = jnp.where(mass > 0, znew, 0.0)
    load = mass * jnp.exp(-rate) * temp
    low = jnp.clip(jnp.floor(znew), 0.0, LEV - 2.0)
    fz = znew - low
    return moved, low, load * (1.0 - fz), load * fz


def load_rows(low, load_lo, load_hi, c):
    lev = iota((LEV, PB), 0, BF)
    a = spread(load_lo, c, LEV, BF)
    b = spread(load_hi, c, LEV, BF)
    rest = jnp.where(lev == spread(low + 1.0, c, LEV, BF), b, jnp.zeros_like(b))
    return jnp.where(lev == spread(low, c, LEV, BF), a, rest)


def bin_rows(low, load_lo, load_hi, col):
    loads = jnp.concatenate([load_rows(low, load_lo, load_hi, c) for c in range(R)], axis=1)
    turned = jnp.concatenate([col, jnp.zeros((PB - R, PB), F32)], axis=0).T.astype(BF)
    lanes = iota((PB, COLS), 1, BF)
    one = jnp.ones((PB, COLS), BF)
    picks = jnp.concatenate(
        [jnp.where(lanes == jnp.broadcast_to(turned[:, c:c + 1], (PB, COLS)), one, jnp.zeros_like(one)) for c in range(R)],
        axis=0)
    return jnp.dot(loads, picks, preferred_element_type=F32)


def group_work(now, before, tperm_ref, val_ref, east):
    fr, height, col = now
    if before is not None:
        moved, b_low, b_lo, b_hi = move(*before, east)
    left = 1.0 - fr
    low = jnp.clip(jnp.floor(height), 0.0, LEV - 2.0)
    odd_i = jnp.floor(low * 0.5)
    even_i = jnp.floor((low + 1.0) * 0.5)
    w_even = jnp.maximum(0.0, 1.0 - jnp.abs(height - 2.0 * even_i))
    w_odd = jnp.maximum(0.0, 1.0 - jnp.abs(height - (2.0 * odd_i + 1.0)))
    g_even = jnp.floor(even_i * 0.125)
    g_odd = jnp.floor(odd_i * 0.125)
    s_even = even_i - 8.0 * g_even
    s_odd = odd_i - 8.0 * g_odd
    col1 = col + 1.0
    ids = iota((COLS, PB), 0, BF)
    sub = iota((8, PB), 0)
    zero = jnp.zeros((COLS, PB), BF)
    for c0 in range(0, R, CH):
        weights = []
        for c in range(c0, c0 + CH):
            rest = jnp.where(ids == spread(col1, c, COLS, BF), spread(fr, c, COLS, BF), zero)
            weights.append(jnp.where(ids == spread(col, c, COLS, BF), spread(left, c, COLS, BF), rest))
        horiz = jnp.dot(tperm_ref[...], jnp.concatenate(weights, axis=1), preferred_element_type=F32)
        for i in range(CH):
            c = c0 + i
            ge = spread(g_even, c, 8)
            go = spread(g_odd, c, 8)
            we = jnp.where(sub == spread(s_even, c, 8), spread(w_even, c, 8), 0.0)
            wo = jnp.where(sub == spread(s_odd, c, 8), spread(w_odd, c, 8), 0.0)
            e_masks = [ge >= float(g) for g in range(1, 8)]
            o_masks = [go >= float(g) for g in range(1, 8)]
            lanes = slice(i * PB, (i + 1) * PB)
            for f in range(4):
                base = f * LEV
                e = horiz[base:base + 8, lanes]
                o = horiz[base + 64:base + 72, lanes]
                for g in range(1, 8):
                    e = jnp.where(e_masks[g - 1], horiz[base + 8 * g:base + 8 * g + 8, lanes], e)
                    o = jnp.where(o_masks[g - 1], horiz[base + 64 + 8 * g:base + 72 + 8 * g, lanes], o)
                val_ref[f, c:c + 1, :] = jnp.sum(e * we + o * wo, axis=0, keepdims=True)
    if before is not None:
        return moved, bin_rows(b_low, b_lo, b_hi, before[4])


def last_group(before, east):
    moved, low, lo, hi = move(*before, east)
    return moved, bin_rows(low, lo, hi, before[4])


def solve(ends, binned, upper_ref, lower_ref, inv_ref, rhs_ref, fwd_ref, back_ref, out_ref):
    top, bot = ends
    half = LEV // 2
    inv = inv_ref[...]
    u, low = upper_ref[...], lower_ref[...]
    upper_rows = lax.broadcasted_iota(jnp.int32, (LEV, COLS), 0) < half
    rhs_ref[...] = binned * inv
    fwd_ref[...] = jnp.where(upper_rows, low, u) * inv
    back_ref[...] = jnp.where(upper_rows, u, low) * inv
    d = rhs_ref[0:1, :]
    e = rhs_ref[LEV - 1:LEV, :]
    ds, es = [d], [e]
    for k in range(1, half):
        m = LEV - 1 - k
        d = rhs_ref[k:k + 1, :] + fwd_ref[k:k + 1, :] * d
        e = rhs_ref[m:m + 1, :] + fwd_ref[m:m + 1, :] * e
        ds.append(d)
        es.append(e)
    kappa = upper_ref[half - 1:half, :]
    alpha = back_ref[half - 1:half, :]
    beta = back_ref[half:half + 1, :]
    det = (kappa * (top + bot) + top * bot) * inv_ref[half - 1:half, :] * inv_ref[half:half + 1, :]
    x = (d + alpha * e) / det
    y = e + beta * x
    out_ref[half - 1:half, :] = x
    out_ref[half:half + 1, :] = y
    for k in range(half - 2, -1, -1):
        m = LEV - 1 - k
        x = ds[k] + back_ref[k:k + 1, :] * x
        y = es[k] + back_ref[m:m + 1, :] * y
        out_ref[k:k + 1, :] = x
        out_ref[m:m + 1, :] = y


N_BAND = 8
N_TILE = 32
NY, NZ = 4, 8
B_DEV = 160
AHEAD = 5
SUB = LEV // N_BAND
ROWS = 32


def offset(i):
    j = (i + NY) // (2 * NY)
    r = (i + NY) % (2 * NY)
    dy = (1 - (j + 7) // 8) * (r % NY) + ((j + 7) // 8) * (r // 2)
    dz = (j + (r % 2) * (NZ - 2 * j)) % NZ
    dz = dz * (1 - j // 4) + 4 * (j // 4)
    dy = dy * (1 - j // 4) + (j // 4) * (r % NY)
    return dy, dz


def place(tile, i, sign):
    dy, dz = offset(i)
    y = (tile // NZ + NY + sign * dy) % NY
    z = (tile % NZ + NZ + sign * dz) % NZ
    return y * NZ + z


def build(dest_ref, parts, col_ref, send_f, send_c):
    dest = dest_ref[...].astype(F32)
    wide = jnp.broadcast_to(dest, (B_DEV, B_DEV))
    row = lax.broadcasted_iota(jnp.int32, (B_DEV, B_DEV), 0)
    lane = lax.broadcasted_iota(jnp.int32, (B_DEV, B_DEV), 1)
    tall = jnp.sum(jnp.where(row == lane, wide, 0.0), axis=1, keepdims=True)
    same = jnp.where((tall == wide) & (row < lane), 1.0, 0.0)
    rank = jnp.sum(same, axis=0, keepdims=True)
    slots = N_TILE * CAP
    pick = jnp.where(iota((slots, B_DEV), 0) == dest * CAP + rank, 1.0, 0.0).astype(BF)
    for f, ref in enumerate(parts[:3]):
        x = ref[...]
        hi = x.astype(BF)
        rest = x - hi.astype(F32)
        mid = rest.astype(BF)
        low = (rest - mid.astype(F32)).astype(BF)
        total = jnp.dot(pick, hi, preferred_element_type=F32)
        total = total + jnp.dot(pick, mid, preferred_element_type=F32)
        total = total + jnp.dot(pick, low, preferred_element_type=F32)
        for t in range(N_TILE):
            send_f[t * ROWS + f * CAP:t * ROWS + (f + 1) * CAP, :] = total[t * CAP:(t + 1) * CAP]
    mass = parts[3][...].astype(BF)
    total = jnp.dot(pick, mass, preferred_element_type=F32)
    for t in range(N_TILE):
        for r in range(2):
            at = t * CAP + 6 + 2 * r
            send_f[t * ROWS + 30 + r:t * ROWS + 31 + r, :] = total[at:at + 1] * 1024.0 + total[at + 1:at + 2]
    rows = iota((N_TILE * 16, B_DEV), 0)
    place16 = dest * 16 + rank
    pick = jnp.where(rows == place16, 1.0, 0.0).astype(BF)
    both = jnp.dot(pick, col_ref[...].astype(F32).astype(BF), preferred_element_type=F32)
    pick = jnp.where(rows == jnp.where(rank < 6.0, place16 + 10.0, -1.0), 1.0, 0.0).astype(BF)
    both = both + jnp.dot(pick, mass, preferred_element_type=F32)
    send_c[...] = both.astype(BF).reshape(N_TILE, 16, PB)


def kernel(wind, temp, diff, removal, frac, height, noise, mass, column, dest,
           conc_ref, moved_ref,
           table, tperm, east_out, east_in, send_f, send_c, recv_f, recv_c,
           in_f, in_c, in_d, val, val_old, binned, upper, lower, inv, rhs, fwd, back,
           field_send, field_recv, own_sem, in_sem, east_sems, f_send, f_recv, c_send, c_recv):
    band, tile = lax.axis_index("band"), lax.axis_index("tile")
    barrier = pltpu.get_barrier_semaphore()

    def greet_tile(i, _):
        pl.semaphore_signal(barrier, inc=1, device_id=(band, place(tile, i, 1)), device_id_type=pl.DeviceIdType.MESH)
        return 0

    def greet_band(i, _):
        pl.semaphore_signal(barrier, inc=1, device_id=((band + i) % N_BAND, tile), device_id_type=pl.DeviceIdType.MESH)
        return 0

    loads = [pltpu.make_async_copy(ref, in_f.at[f], in_sem.at[f]) for f, ref in enumerate((frac, height, noise, mass))]
    loads.append(pltpu.make_async_copy(column, in_c, in_sem.at[4]))
    loads.append(pltpu.make_async_copy(dest, in_d, in_sem.at[5]))
    for copy in loads:
        copy.start()
    lax.fori_loop(1, N_TILE, greet_tile, 0)
    lax.fori_loop(1, N_BAND, greet_band, 0)
    fields = (wind, temp, diff, removal)
    own = [pltpu.make_async_copy(ref.at[band], table.at[pl.ds(pl.multiple_of(f * LEV + band * SUB, SUB), SUB)], own_sem.at[f])
           for f, ref in enumerate(fields)]
    for copy in own:
        copy.start()
    for copy in loads:
        copy.wait()
    build(in_d, [in_f.at[f] for f in range(4)], in_c, send_f, send_c)
    pl.semaphore_wait(barrier, N_TILE + N_BAND - 2)

    def field_copy(i, f, to, rows_of):
        return pltpu.make_async_remote_copy(
            src_ref=fields[f].at[to], dst_ref=table.at[pl.ds(pl.multiple_of(f * LEV + rows_of * SUB, SUB), SUB)],
            send_sem=field_send.at[i, f], recv_sem=field_recv.at[i, f],
            device_id=(to, tile), device_id_type=pl.DeviceIdType.MESH)

    def record_copies(i):
        to = place(tile, i, 1)
        return [pltpu.make_async_remote_copy(
            src_ref=send_f.at[pl.ds(pl.multiple_of(to * ROWS, 8), ROWS)], dst_ref=recv_f.at[i // G, pl.ds(pl.multiple_of(i % G * ROWS, 8), ROWS)],
            send_sem=f_send.at[i], recv_sem=f_recv.at[i],
            device_id=(band, to), device_id_type=pl.DeviceIdType.MESH),
            pltpu.make_async_remote_copy(
            src_ref=send_c.at[to], dst_ref=recv_c.at[i],
            send_sem=c_send.at[i], recv_sem=c_recv.at[i],
            device_id=(band, to), device_id_type=pl.DeviceIdType.MESH)]

    def send_fields(i, _):
        to = (band + i) % N_BAND
        for f in range(4):
            field_copy(i, f, to, band).start()
        return 0

    def send_records(i, _):
        for copy in record_copies(i):
            copy.start()
        return 0

    lax.fori_loop(1, AHEAD * G, send_records, 0)
    lax.fori_loop(1, N_BAND, send_fields, 0)
    recv_f[0, 0:ROWS, :] = send_f[pl.ds(pl.multiple_of(tile * ROWS, 8), ROWS), :]
    recv_c[0] = send_c[tile]
    binned[...] = jnp.zeros_like(binned)
    for copy in own:
        copy.wait()

    def take_fields(i, _):
        source = (band + N_BAND - i) % N_BAND
        for f in range(4):
            field_copy(i, f, (band + i) % N_BAND, source).wait_recv()
        return 0

    lax.fori_loop(1, N_BAND, take_fields, 0)
    first = jnp.where(lax.broadcasted_iota(jnp.int32, (8, COLS), 1) == 0, 1.0, 0.0).astype(BF)
    east_out[...] = lax.dot_general(first, table[...], (((1,), (1,)), ((), ())), preferred_element_type=F32)
    west = (tile + N_TILE - 1) % N_TILE
    east_copy = pltpu.make_async_remote_copy(
        src_ref=east_out, dst_ref=east_in, send_sem=east_sems.at[0], recv_sem=east_sems.at[1],
        device_id=(band, west), device_id_type=pl.DeviceIdType.MESH)
    east_copy.start()
    split_levels(table, tperm)
    set_kappa(table, upper, lower)
    def take_records(i, _):
        for copy in record_copies(i):
            copy.wait_recv()
        return 0

    def rows_of(q):
        return [jnp.concatenate([recv_f[q, j * ROWS + f * CAP:j * ROWS + (f + 1) * CAP, :] for j in range(G)], axis=0)
                for f in range(3)]

    def col_of(q):
        return jnp.concatenate([recv_c[q * G + j].astype(F32)[:CAP] for j in range(G)], axis=0)

    def mass_of(q):
        out = []
        for j in range(G):
            out.append(recv_c[q * G + j].astype(F32)[CAP:])
            for r in range(2):
                pair = recv_f[q, j * ROWS + 30 + r:j * ROWS + 31 + r, :]
                even = jnp.floor(pair * 0.25) * (1.0 / 256.0)
                out += [even, pair - even * 1024.0]
        return jnp.concatenate(out, axis=0)

    def before_of(q):
        return (*rows_of(q), mass_of(q), col_of(q), [val_old[f] for f in range(4)])

    def put(q, moved):
        for j in range(G):
            moved_ref[pl.ds(place(tile, q * G + j, -1) * CAP, CAP), :] = moved[j * CAP:(j + 1) * CAP]

    lax.fori_loop(1, G, take_records, 0)
    one = jnp.ones((1, COLS), F32)
    carry = pivots(0, (one, one), upper, lower, inv)
    fr, h, _ = rows_of(0)
    group_work((fr, h, col_of(0)), None, tperm, val_old, None)
    east_copy.wait()
    east = [east_in[:, f * LEV:(f + 1) * LEV] for f in range(4)]

    def body(q, carry):
        lax.fori_loop(q * G, q * G + G, take_records, 0)
        first = jnp.minimum((q + AHEAD - 1) * G, N_TILE)
        lax.fori_loop(first, jnp.minimum(first + G, N_TILE), send_records, 0)
        carry, ends = pivots(q, carry[0], upper, lower, inv)
        fr, h, _ = rows_of(q)
        moved, bins = group_work((fr, h, col_of(q)), before_of(q - 1), tperm, val, east)
        put(q - 1, moved)
        binned[...] += bins
        val_old[...] = val[...]
        return carry, ends

    _, ends = lax.fori_loop(1, NG, body, carry)
    moved, bins = last_group(before_of(NG - 1), east)
    put(NG - 1, moved)
    solve(ends, binned[...] + bins, upper, lower, inv, rhs, fwd, back, conc_ref)

    def sent_fields(i, _):
        for f in range(4):
            field_copy(i, f, (band + i) % N_BAND, band).wait_send()
        return 0

    def sent_records(i, _):
        for copy in record_copies(i):
            copy.wait_send()
        return 0

    lax.fori_loop(1, N_BAND, sent_fields, 0)
    lax.fori_loop(1, N_TILE, sent_records, 0)


def shards(wind, temp, diff, removal, frac, height, mass, noise, column, dest):
    vm = pl.BlockSpec(memory_space=pltpu.VMEM)
    hbm = pl.BlockSpec(memory_space=pltpu.HBM)
    grid = pltpu.VMEM((LEV, COLS), F32)
    dma = pltpu.SemaphoreType.DMA
    conc, moved = pl.pallas_call(
        kernel,
        out_shape=(jax.ShapeDtypeStruct((LEV, COLS), F32), jax.ShapeDtypeStruct((N_TILE * CAP, PB), F32)),
        in_specs=[hbm] * 10,
        out_specs=(vm, vm),
        scratch_shapes=[
            pltpu.VMEM((4 * LEV, COLS), BF), pltpu.VMEM((4 * LEV, COLS), BF),
            pltpu.VMEM((8, 4 * LEV), F32), pltpu.VMEM((8, 4 * LEV), F32),
            pltpu.VMEM((N_TILE * ROWS, PB), F32), pltpu.VMEM((N_TILE, 16, PB), BF),
            pltpu.VMEM((NG, G * ROWS, PB), F32), pltpu.VMEM((N_TILE, 16, PB), BF),
            pltpu.VMEM((4, B_DEV, PB), F32), pltpu.VMEM((B_DEV, PB), jnp.int32), pltpu.VMEM((1, B_DEV), jnp.int32),
            pltpu.VMEM((4, R, PB), F32), pltpu.VMEM((4, R, PB), F32), grid,
            grid, grid, grid, grid, grid, grid,
            dma((N_BAND, 4)), dma((N_BAND, 4)), dma((4,)), dma((6,)), dma((2,)),
            dma((N_TILE,)), dma((N_TILE,)), dma((N_TILE,)), dma((N_TILE,)),
        ],
        compiler_params=pltpu.CompilerParams(
            collective_id=0, has_side_effects=True, vmem_limit_bytes=63 * 2**20),
        cost_estimate=pl.CostEstimate(flops=2 * 40960 * 256 * 640, bytes_accessed=2 * 2**20, transcendentals=0),
    )(wind, temp, diff, removal, frac, height, noise, mass, column, dest.reshape(1, B_DEV))
    return conc[None], moved


def solution(mesh):
    read = P(None, "band", "tile")
    rec = P(("band", "tile"), None)
    return jax.shard_map(
        shards, mesh=mesh,
        in_specs=(read,) * 4 + (rec,) * 5 + (P(("band", "tile")),),
        out_specs=(P("band", None, "tile"), rec), check_vma=False)
```

```python
import jax
import jax.numpy as jnp
from jax import lax
from jax.experimental import pallas as pl
from jax.experimental.pallas import tpu as pltpu
from jax.sharding import PartitionSpec as P

LEV = 128
COLS = 256
CAP = 10
PB = 128
CH = 2
F32 = jnp.float32
BF = jnp.bfloat16


def iota(shape, dim, dtype=F32):
    return lax.broadcasted_iota(jnp.int32, shape, dim).astype(dtype)


def split_levels(table_ref, tperm_ref):
    row = lax.broadcasted_iota(jnp.int32, (LEV, LEV), 0)
    col = lax.broadcasted_iota(jnp.int32, (LEV, LEV), 1)
    source = jnp.where(row < LEV // 2, 2 * row, 2 * row - (LEV - 1))
    perm = (col == source).astype(F32).astype(BF)
    for f in range(4):
        part = pl.ds(f * LEV, LEV)
        tperm_ref[part, :] = jnp.dot(perm, table_ref[part, :], preferred_element_type=F32).astype(BF)


def set_kappa(table_ref, upper_ref, lower_ref):
    k = table_ref[pl.ds(2 * LEV, LEV), :].astype(F32)
    kappa = 0.5 * (k[:-1] + k[1:])
    zero = jnp.zeros((1, COLS), F32)
    upper_ref[...] = jnp.concatenate([kappa, zero], axis=0)
    lower_ref[...] = jnp.concatenate([zero, kappa], axis=0)


def pivots(step, carry, upper_ref, lower_ref, inv_ref):
    top, bot = carry
    for i in range(LEV // 2 // NG):
        k = LEV // 2 // NG * step + i
        u = upper_ref[pl.ds(k, 1), :]
        inv = 1.0 / (top + u)
        inv_ref[pl.ds(k, 1), :] = inv
        last_top = top
        top = 1.0 + u * (top * inv)
        m = LEV - 1 - k
        low = lower_ref[pl.ds(m, 1), :]
        inv = 1.0 / (bot + low)
        inv_ref[pl.ds(m, 1), :] = inv
        last_bot = bot
        bot = 1.0 + low * (bot * inv)
    return (top, bot), (last_top, last_bot)


G = 4
NG = 8
R = G * CAP


def spread(x, c, rows, dtype=F32):
    return jnp.broadcast_to(x[c:c + 1], (rows, PB)).astype(dtype)


def move(fr, height, noise, mass, col, val, east):
    low = jnp.clip(jnp.floor(height), 0.0, LEV - 2.0)
    fz = height - low
    right = fr.astype(BF).astype(F32)
    edge = jnp.where(col == COLS - 1.0, right, 0.0)
    low_i = low.astype(jnp.int32)

    def picked(table, index):
        return jnp.concatenate([jnp.take_along_axis(table, index[r:r + 8], axis=1) for r in range(0, R, 8)], axis=0)

    w, temp, kd, rate = [
        val[f] + edge * (picked(east[f], low_i) * (1.0 - fz) + picked(east[f], low_i + 1) * fz) for f in range(4)]
    znew = jnp.clip(height + w + jnp.sqrt(2.0 * kd) * noise, 0.0, LEV - 1.0)
    moved = jnp.where(mass > 0, znew, 0.0)
    load = mass * jnp.exp(-rate) * temp
    low = jnp.clip(jnp.floor(znew), 0.0, LEV - 2.0)
    fz = znew - low
    return moved, low, load * (1.0 - fz), load * fz


def load_rows(low, load_lo, load_hi, c):
    lev = iota((LEV, PB), 0, BF)
    a = spread(load_lo, c, LEV, BF)
    b = spread(load_hi, c, LEV, BF)
    rest = jnp.where(lev == spread(low + 1.0, c, LEV, BF), b, jnp.zeros_like(b))
    return jnp.where(lev == spread(low, c, LEV, BF), a, rest)


def bin_rows(low, load_lo, load_hi, col):
    loads = jnp.concatenate([load_rows(low, load_lo, load_hi, c) for c in range(R)], axis=1)
    turned = jnp.concatenate([col, jnp.zeros((PB - R, PB), F32)], axis=0).T.astype(BF)
    lanes = iota((PB, COLS), 1, BF)
    one = jnp.ones((PB, COLS), BF)
    picks = jnp.concatenate(
        [jnp.where(lanes == jnp.broadcast_to(turned[:, c:c + 1], (PB, COLS)), one, jnp.zeros_like(one)) for c in range(R)],
        axis=0)
    return jnp.dot(loads, picks, preferred_element_type=F32)


def group_work(now, before, tperm_ref, val_ref, east):
    fr, height, col = now
    if before is not None:
        moved, b_low, b_lo, b_hi = move(*before, east)
    left = 1.0 - fr
    low = jnp.clip(jnp.floor(height), 0.0, LEV - 2.0)
    odd_i = jnp.floor(low * 0.5)
    even_i = jnp.floor((low + 1.0) * 0.5)
    w_even = jnp.maximum(0.0, 1.0 - jnp.abs(height - 2.0 * even_i))
    w_odd = jnp.maximum(0.0, 1.0 - jnp.abs(height - (2.0 * odd_i + 1.0)))
    g_even = jnp.floor(even_i * 0.125)
    g_odd = jnp.floor(odd_i * 0.125)
    s_even = even_i - 8.0 * g_even
    s_odd = odd_i - 8.0 * g_odd
    col1 = col + 1.0
    ids = iota((COLS, PB), 0, BF)
    sub = iota((8, PB), 0)
    zero = jnp.zeros((COLS, PB), BF)
    for c0 in range(0, R, CH):
        weights = []
        for c in range(c0, c0 + CH):
            rest = jnp.where(ids == spread(col1, c, COLS, BF), spread(fr, c, COLS, BF), zero)
            weights.append(jnp.where(ids == spread(col, c, COLS, BF), spread(left, c, COLS, BF), rest))
        horiz = jnp.dot(tperm_ref[...], jnp.concatenate(weights, axis=1), preferred_element_type=F32)
        for i in range(CH):
            c = c0 + i
            ge = spread(g_even, c, 8)
            go = spread(g_odd, c, 8)
            we = jnp.where(sub == spread(s_even, c, 8), spread(w_even, c, 8), 0.0)
            wo = jnp.where(sub == spread(s_odd, c, 8), spread(w_odd, c, 8), 0.0)
            e_masks = [ge >= float(g) for g in range(1, 8)]
            o_masks = [go >= float(g) for g in range(1, 8)]
            lanes = slice(i * PB, (i + 1) * PB)
            for f in range(4):
                base = f * LEV
                e = horiz[base:base + 8, lanes]
                o = horiz[base + 64:base + 72, lanes]
                for g in range(1, 8):
                    e = jnp.where(e_masks[g - 1], horiz[base + 8 * g:base + 8 * g + 8, lanes], e)
                    o = jnp.where(o_masks[g - 1], horiz[base + 64 + 8 * g:base + 72 + 8 * g, lanes], o)
                val_ref[f, c:c + 1, :] = jnp.sum(e * we + o * wo, axis=0, keepdims=True)
    if before is not None:
        return moved, bin_rows(b_low, b_lo, b_hi, before[4])


def last_group(before, east):
    moved, low, lo, hi = move(*before, east)
    return moved, bin_rows(low, lo, hi, before[4])


def solve(ends, binned, upper_ref, lower_ref, inv_ref, rhs_ref, fwd_ref, back_ref, out_ref):
    top, bot = ends
    half = LEV // 2
    inv = inv_ref[...]
    u, low = upper_ref[...], lower_ref[...]
    upper_rows = lax.broadcasted_iota(jnp.int32, (LEV, COLS), 0) < half
    rhs_ref[...] = binned * inv
    fwd_ref[...] = jnp.where(upper_rows, low, u) * inv
    back_ref[...] = jnp.where(upper_rows, u, low) * inv
    d = rhs_ref[0:1, :]
    e = rhs_ref[LEV - 1:LEV, :]
    ds, es = [d], [e]
    for k in range(1, half):
        m = LEV - 1 - k
        d = rhs_ref[k:k + 1, :] + fwd_ref[k:k + 1, :] * d
        e = rhs_ref[m:m + 1, :] + fwd_ref[m:m + 1, :] * e
        ds.append(d)
        es.append(e)
    kappa = upper_ref[half - 1:half, :]
    alpha = back_ref[half - 1:half, :]
    beta = back_ref[half:half + 1, :]
    det = (kappa * (top + bot) + top * bot) * inv_ref[half - 1:half, :] * inv_ref[half:half + 1, :]
    x = (d + alpha * e) / det
    y = e + beta * x
    out_ref[half - 1:half, :] = x
    out_ref[half:half + 1, :] = y
    for k in range(half - 2, -1, -1):
        m = LEV - 1 - k
        x = ds[k] + back_ref[k:k + 1, :] * x
        y = es[k] + back_ref[m:m + 1, :] * y
        out_ref[k:k + 1, :] = x
        out_ref[m:m + 1, :] = y


N_BAND = 8
N_TILE = 32
NY, NZ = 4, 8
B_DEV = 160
AHEAD = 5
SUB = LEV // N_BAND
ROWS = 32


def offset(i):
    j = (i + NY) // (2 * NY)
    r = (i + NY) % (2 * NY)
    dy = (1 - (j + 7) // 8) * (r % NY) + ((j + 7) // 8) * (r // 2)
    dz = (j + (r % 2) * (NZ - 2 * j)) % NZ
    dz = dz * (1 - j // 4) + 4 * (j // 4)
    dy = dy * (1 - j // 4) + (j // 4) * (r % NY)
    return dy, dz


def place(tile, i, sign):
    dy, dz = offset(i)
    y = (tile // NZ + NY + sign * dy) % NY
    z = (tile % NZ + NZ + sign * dz) % NZ
    return y * NZ + z


def build(dest_ref, parts, col_ref, send_f, send_c):
    dest = dest_ref[...].astype(F32)
    wide = jnp.broadcast_to(dest, (B_DEV, B_DEV))
    row = lax.broadcasted_iota(jnp.int32, (B_DEV, B_DEV), 0)
    lane = lax.broadcasted_iota(jnp.int32, (B_DEV, B_DEV), 1)
    tall = jnp.sum(jnp.where(row == lane, wide, 0.0), axis=1, keepdims=True)
    same = jnp.where((tall == wide) & (row < lane), 1.0, 0.0)
    rank = jnp.sum(same, axis=0, keepdims=True)
    slots = N_TILE * CAP
    pick = jnp.where(iota((slots, B_DEV), 0) == dest * CAP + rank, 1.0, 0.0).astype(BF)
    for f, ref in enumerate(parts[:3]):
        x = ref[...]
        hi = x.astype(BF)
        rest = x - hi.astype(F32)
        mid = rest.astype(BF)
        low = (rest - mid.astype(F32)).astype(BF)
        total = jnp.dot(pick, hi, preferred_element_type=F32)
        total = total + jnp.dot(pick, mid, preferred_element_type=F32)
        total = total + jnp.dot(pick, low, preferred_element_type=F32)
        for t in range(N_TILE):
            send_f[t * ROWS + f * CAP:t * ROWS + (f + 1) * CAP, :] = total[t * CAP:(t + 1) * CAP]
    mass = parts[3][...].astype(BF)
    total = jnp.dot(pick, mass, preferred_element_type=F32)
    for t in range(N_TILE):
        for r in range(2):
            at = t * CAP + 6 + 2 * r
            send_f[t * ROWS + 30 + r:t * ROWS + 31 + r, :] = total[at:at + 1] * 1024.0 + total[at + 1:at + 2]
    rows = iota((N_TILE * 16, B_DEV), 0)
    place16 = dest * 16 + rank
    pick = jnp.where(rows == place16, 1.0, 0.0).astype(BF)
    both = jnp.dot(pick, col_ref[...].astype(F32).astype(BF), preferred_element_type=F32)
    pick = jnp.where(rows == jnp.where(rank < 6.0, place16 + 10.0, -1.0), 1.0, 0.0).astype(BF)
    both = both + jnp.dot(pick, mass, preferred_element_type=F32)
    send_c[...] = both.astype(BF).reshape(N_TILE, 16, PB)


def kernel(wind, temp, diff, removal, frac, height, noise, mass, column, dest,
           conc_ref, moved_ref,
           table, tperm, east_out, east_in, send_f, send_c, recv_f, recv_c,
           in_f, in_c, in_d, val, val_old, binned, upper, lower, inv, rhs, fwd, back,
           field_send, field_recv, own_sem, in_sem, east_sems, f_send, f_recv, c_send, c_recv):
    band, tile = lax.axis_index("band"), lax.axis_index("tile")
    barrier = pltpu.get_barrier_semaphore()

    def greet_tile(i, _):
        pl.semaphore_signal(barrier, inc=1, device_id=(band, place(tile, i, 1)), device_id_type=pl.DeviceIdType.MESH)
        return 0

    def greet_band(i, _):
        pl.semaphore_signal(barrier, inc=1, device_id=((band + i) % N_BAND, tile), device_id_type=pl.DeviceIdType.MESH)
        return 0

    loads = [pltpu.make_async_copy(ref, in_f.at[f], in_sem.at[f]) for f, ref in enumerate((frac, height, noise, mass))]
    loads.append(pltpu.make_async_copy(column, in_c, in_sem.at[4]))
    loads.append(pltpu.make_async_copy(dest, in_d, in_sem.at[5]))
    for copy in loads:
        copy.start()
    lax.fori_loop(1, N_TILE, greet_tile, 0)
    lax.fori_loop(1, N_BAND, greet_band, 0)
    fields = (wind, temp, diff, removal)
    own = [pltpu.make_async_copy(ref.at[band], table.at[pl.ds(pl.multiple_of(f * LEV + band * SUB, SUB), SUB)], own_sem.at[f])
           for f, ref in enumerate(fields)]
    for copy in own:
        copy.start()
    for copy in loads:
        copy.wait()
    build(in_d, [in_f.at[f] for f in range(4)], in_c, send_f, send_c)
    pl.semaphore_wait(barrier, N_TILE + N_BAND - 2)

    def field_copy(i, f, to, rows_of):
        return pltpu.make_async_remote_copy(
            src_ref=fields[f].at[to], dst_ref=table.at[pl.ds(pl.multiple_of(f * LEV + rows_of * SUB, SUB), SUB)],
            send_sem=field_send.at[i, f], recv_sem=field_recv.at[i, f],
            device_id=(to, tile), device_id_type=pl.DeviceIdType.MESH)

    def record_copies(i):
        to = place(tile, i, 1)
        return [pltpu.make_async_remote_copy(
            src_ref=send_f.at[pl.ds(pl.multiple_of(to * ROWS, 8), ROWS)], dst_ref=recv_f.at[i // G, pl.ds(pl.multiple_of(i % G * ROWS, 8), ROWS)],
            send_sem=f_send.at[i], recv_sem=f_recv.at[i],
            device_id=(band, to), device_id_type=pl.DeviceIdType.MESH),
            pltpu.make_async_remote_copy(
            src_ref=send_c.at[to], dst_ref=recv_c.at[i],
            send_sem=c_send.at[i], recv_sem=c_recv.at[i],
            device_id=(band, to), device_id_type=pl.DeviceIdType.MESH)]

    def send_fields(i, _):
        to = (band + i) % N_BAND
        for f in range(4):
            field_copy(i, f, to, band).start()
        return 0

    def send_records(i, _):
        for copy in record_copies(i):
            copy.start()
        return 0

    lax.fori_loop(1, N_BAND, send_fields, 0)
    lax.fori_loop(1, AHEAD * G, send_records, 0)
    recv_f[0, 0:ROWS, :] = send_f[pl.ds(pl.multiple_of(tile * ROWS, 8), ROWS), :]
    recv_c[0] = send_c[tile]
    binned[...] = jnp.zeros_like(binned)
    for copy in own:
        copy.wait()

    def take_fields(i, _):
        source = (band + N_BAND - i) % N_BAND
        for f in range(4):
            field_copy(i, f, (band + i) % N_BAND, source).wait_recv()
        return 0

    lax.fori_loop(1, N_BAND, take_fields, 0)
    first = jnp.where(lax.broadcasted_iota(jnp.int32, (8, COLS), 1) == 0, 1.0, 0.0).astype(BF)
    east_out[...] = lax.dot_general(first, table[...], (((1,), (1,)), ((), ())), preferred_element_type=F32)
    west = (tile + N_TILE - 1) % N_TILE
    east_copy = pltpu.make_async_remote_copy(
        src_ref=east_out, dst_ref=east_in, send_sem=east_sems.at[0], recv_sem=east_sems.at[1],
        device_id=(band, west), device_id_type=pl.DeviceIdType.MESH)
    east_copy.start()
    split_levels(table, tperm)
    set_kappa(table, upper, lower)
    def take_records(i, _):
        for copy in record_copies(i):
            copy.wait_recv()
        return 0

    def rows_of(q):
        return [jnp.concatenate([recv_f[q, j * ROWS + f * CAP:j * ROWS + (f + 1) * CAP, :] for j in range(G)], axis=0)
                for f in range(3)]

    def col_of(q):
        return jnp.concatenate([recv_c[q * G + j].astype(F32)[:CAP] for j in range(G)], axis=0)

    def mass_of(q):
        out = []
        for j in range(G):
            out.append(recv_c[q * G + j].astype(F32)[CAP:])
            for r in range(2):
                pair = recv_f[q, j * ROWS + 30 + r:j * ROWS + 31 + r, :]
                even = jnp.floor(pair * 0.25) * (1.0 / 256.0)
                out += [even, pair - even * 1024.0]
        return jnp.concatenate(out, axis=0)

    def before_of(q):
        return (*rows_of(q), mass_of(q), col_of(q), [val_old[f] for f in range(4)])

    def put(q, moved):
        for j in range(G):
            moved_ref[pl.ds(place(tile, q * G + j, -1) * CAP, CAP), :] = moved[j * CAP:(j + 1) * CAP]

    lax.fori_loop(1, G, take_records, 0)
    one = jnp.ones((1, COLS), F32)
    carry = pivots(0, (one, one), upper, lower, inv)
    fr, h, _ = rows_of(0)
    group_work((fr, h, col_of(0)), None, tperm, val_old, None)
    east_copy.wait()
    east = [east_in[:, f * LEV:(f + 1) * LEV] for f in range(4)]

    def body(q, carry):
        lax.fori_loop(q * G, q * G + G, take_records, 0)
        first = jnp.minimum((q + AHEAD - 1) * G, N_TILE)
        lax.fori_loop(first, jnp.minimum(first + G, N_TILE), send_records, 0)
        carry, ends = pivots(q, carry[0], upper, lower, inv)
        fr, h, _ = rows_of(q)
        moved, bins = group_work((fr, h, col_of(q)), before_of(q - 1), tperm, val, east)
        put(q - 1, moved)
        binned[...] += bins
        val_old[...] = val[...]
        return carry, ends

    _, ends = lax.fori_loop(1, NG, body, carry)
    moved, bins = last_group(before_of(NG - 1), east)
    put(NG - 1, moved)
    solve(ends, binned[...] + bins, upper, lower, inv, rhs, fwd, back, conc_ref)

    def sent_fields(i, _):
        for f in range(4):
            field_copy(i, f, (band + i) % N_BAND, band).wait_send()
        return 0

    def sent_records(i, _):
        for copy in record_copies(i):
            copy.wait_send()
        return 0

    lax.fori_loop(1, N_BAND, sent_fields, 0)
    lax.fori_loop(1, N_TILE, sent_records, 0)


def hand_on(conc_in, moved_in, conc_out, moved_out, conc, moved, sem):
    ins = [pltpu.make_async_copy(moved_in, moved, sem.at[0]), pltpu.make_async_copy(conc_in, conc, sem.at[1])]
    outs = [pltpu.make_async_copy(moved, moved_out, sem.at[2]), pltpu.make_async_copy(conc, conc_out, sem.at[3])]
    for copy in ins:
        copy.start()
    for before, after in zip(ins, outs):
        before.wait()
        after.start()
    for copy in outs:
        copy.wait()


def shards(wind, temp, diff, removal, frac, height, mass, noise, column, dest):
    vm = pl.BlockSpec(memory_space=pltpu.VMEM)
    hbm = pl.BlockSpec(memory_space=pltpu.HBM)
    grid = pltpu.VMEM((LEV, COLS), F32)
    dma = pltpu.SemaphoreType.DMA
    conc, moved = pl.pallas_call(
        kernel,
        out_shape=(jax.ShapeDtypeStruct((LEV, COLS), F32), jax.ShapeDtypeStruct((N_TILE * CAP, PB), F32)),
        in_specs=[hbm] * 10,
        out_specs=(vm, vm),
        scratch_shapes=[
            pltpu.VMEM((4 * LEV, COLS), BF), pltpu.VMEM((4 * LEV, COLS), BF),
            pltpu.VMEM((8, 4 * LEV), F32), pltpu.VMEM((8, 4 * LEV), F32),
            pltpu.VMEM((N_TILE * ROWS, PB), F32), pltpu.VMEM((N_TILE, 16, PB), BF),
            pltpu.VMEM((NG, G * ROWS, PB), F32), pltpu.VMEM((N_TILE, 16, PB), BF),
            pltpu.VMEM((4, B_DEV, PB), F32), pltpu.VMEM((B_DEV, PB), jnp.int32), pltpu.VMEM((1, B_DEV), jnp.int32),
            pltpu.VMEM((4, R, PB), F32), pltpu.VMEM((4, R, PB), F32), grid,
            grid, grid, grid, grid, grid, grid,
            dma((N_BAND, 4)), dma((N_BAND, 4)), dma((4,)), dma((6,)), dma((2,)),
            dma((N_TILE,)), dma((N_TILE,)), dma((N_TILE,)), dma((N_TILE,)),
        ],
        compiler_params=pltpu.CompilerParams(
            collective_id=0, has_side_effects=True, vmem_limit_bytes=63 * 2**20),
        cost_estimate=pl.CostEstimate(flops=2 * 40960 * 256 * 640, bytes_accessed=2 * 2**20, transcendentals=0),
    )(wind, temp, diff, removal, frac, height, noise, mass, column, dest.reshape(1, B_DEV))
    conc, moved = pl.pallas_call(
        hand_on,
        out_shape=(jax.ShapeDtypeStruct((LEV, COLS), F32), jax.ShapeDtypeStruct((N_TILE * CAP, PB), F32)),
        in_specs=[hbm] * 2, out_specs=(hbm, hbm),
        scratch_shapes=[grid, pltpu.VMEM((N_TILE * CAP, PB), F32), dma((4,))],
        compiler_params=pltpu.CompilerParams(vmem_limit_bytes=63 * 2**20),
    )(conc, moved)
    return conc[None], moved


def solution(mesh):
    read = P(None, "band", "tile")
    rec = P(("band", "tile"), None)
    return jax.shard_map(
        shards, mesh=mesh,
        in_specs=(read,) * 4 + (rec,) * 5 + (P(("band", "tile")),),
        out_specs=(P("band", None, "tile"), rec), check_vma=False)
```

```python
import jax
import jax.numpy as jnp
from jax import lax
from jax.experimental import pallas as pl
from jax.experimental.pallas import tpu as pltpu
from jax.sharding import PartitionSpec as P

LEV = 128
COLS = 256
CAP = 10
PB = 128
CH = 2
F32 = jnp.float32
BF = jnp.bfloat16


def iota(shape, dim, dtype=F32):
    return lax.broadcasted_iota(jnp.int32, shape, dim).astype(dtype)


def split_levels(table_ref, tperm_ref):
    row = lax.broadcasted_iota(jnp.int32, (LEV, LEV), 0)
    col = lax.broadcasted_iota(jnp.int32, (LEV, LEV), 1)
    source = jnp.where(row < LEV // 2, 2 * row, 2 * row - (LEV - 1))
    perm = (col == source).astype(F32).astype(BF)
    for f in range(4):
        part = pl.ds(f * LEV, LEV)
        tperm_ref[part, :] = jnp.dot(perm, table_ref[part, :], preferred_element_type=F32).astype(BF)


def set_kappa(table_ref, upper_ref, lower_ref):
    k = table_ref[pl.ds(2 * LEV, LEV), :].astype(F32)
    kappa = 0.5 * (k[:-1] + k[1:])
    zero = jnp.zeros((1, COLS), F32)
    upper_ref[...] = jnp.concatenate([kappa, zero], axis=0)
    lower_ref[...] = jnp.concatenate([zero, kappa], axis=0)


def pivots(step, carry, upper_ref, lower_ref, inv_ref):
    top, bot = carry
    for i in range(LEV // 2 // NG):
        k = LEV // 2 // NG * step + i
        u = upper_ref[pl.ds(k, 1), :]
        inv = 1.0 / (top + u)
        inv_ref[pl.ds(k, 1), :] = inv
        last_top = top
        top = 1.0 + u * (top * inv)
        m = LEV - 1 - k
        low = lower_ref[pl.ds(m, 1), :]
        inv = 1.0 / (bot + low)
        inv_ref[pl.ds(m, 1), :] = inv
        last_bot = bot
        bot = 1.0 + low * (bot * inv)
    return (top, bot), (last_top, last_bot)


G = 4
NG = 8
R = G * CAP


def spread(x, c, rows, dtype=F32):
    return jnp.broadcast_to(x[c:c + 1], (rows, PB)).astype(dtype)


def move(fr, height, noise, mass, col, val, east):
    low = jnp.clip(jnp.floor(height), 0.0, LEV - 2.0)
    fz = height - low
    right = fr.astype(BF).astype(F32)
    edge = jnp.where(col == COLS - 1.0, right, 0.0)
    low_i = low.astype(jnp.int32)

    def picked(table, index):
        return jnp.concatenate([jnp.take_along_axis(table, index[r:r + 8], axis=1) for r in range(0, R, 8)], axis=0)

    w, temp, kd, rate = [
        val[f] + edge * (picked(east[f], low_i) * (1.0 - fz) + picked(east[f], low_i + 1) * fz) for f in range(4)]
    znew = jnp.clip(height + w + jnp.sqrt(2.0 * kd) * noise, 0.0, LEV - 1.0)
    moved = jnp.where(mass > 0, znew, 0.0)
    load = mass * jnp.exp(-rate) * temp
    low = jnp.clip(jnp.floor(znew), 0.0, LEV - 2.0)
    fz = znew - low
    return moved, low, load * (1.0 - fz), load * fz


def load_rows(low, load_lo, load_hi, c):
    lev = iota((LEV, PB), 0, BF)
    a = spread(load_lo, c, LEV, BF)
    b = spread(load_hi, c, LEV, BF)
    rest = jnp.where(lev == spread(low + 1.0, c, LEV, BF), b, jnp.zeros_like(b))
    return jnp.where(lev == spread(low, c, LEV, BF), a, rest)


def bin_rows(low, load_lo, load_hi, col):
    loads = jnp.concatenate([load_rows(low, load_lo, load_hi, c) for c in range(R)], axis=1)
    turned = jnp.concatenate([col, jnp.zeros((PB - R, PB), F32)], axis=0).T.astype(BF)
    lanes = iota((PB, COLS), 1, BF)
    one = jnp.ones((PB, COLS), BF)
    picks = jnp.concatenate(
        [jnp.where(lanes == jnp.broadcast_to(turned[:, c:c + 1], (PB, COLS)), one, jnp.zeros_like(one)) for c in range(R)],
        axis=0)
    return jnp.dot(loads, picks, preferred_element_type=F32)


def group_work(now, before, tperm_ref, val_ref, east):
    fr, height, col = now
    if before is not None:
        moved, b_low, b_lo, b_hi = move(*before, east)
    left = 1.0 - fr
    low = jnp.clip(jnp.floor(height), 0.0, LEV - 2.0)
    odd_i = jnp.floor(low * 0.5)
    even_i = jnp.floor((low + 1.0) * 0.5)
    w_even = jnp.maximum(0.0, 1.0 - jnp.abs(height - 2.0 * even_i))
    w_odd = jnp.maximum(0.0, 1.0 - jnp.abs(height - (2.0 * odd_i + 1.0)))
    g_even = jnp.floor(even_i * 0.125)
    g_odd = jnp.floor(odd_i * 0.125)
    s_even = even_i - 8.0 * g_even
    s_odd = odd_i - 8.0 * g_odd
    col1 = col + 1.0
    ids = iota((COLS, PB), 0, BF)
    sub = iota((8, PB), 0)
    zero = jnp.zeros((COLS, PB), BF)
    for c0 in range(0, R, CH):
        weights = []
        for c in range(c0, c0 + CH):
            rest = jnp.where(ids == spread(col1, c, COLS, BF), spread(fr, c, COLS, BF), zero)
            weights.append(jnp.where(ids == spread(col, c, COLS, BF), spread(left, c, COLS, BF), rest))
        horiz = jnp.dot(tperm_ref[...], jnp.concatenate(weights, axis=1), preferred_element_type=F32)
        for i in range(CH):
            c = c0 + i
            ge = spread(g_even, c, 8)
            go = spread(g_odd, c, 8)
            we = jnp.where(sub == spread(s_even, c, 8), spread(w_even, c, 8), 0.0)
            wo = jnp.where(sub == spread(s_odd, c, 8), spread(w_odd, c, 8), 0.0)
            e_masks = [ge >= float(g) for g in range(1, 8)]
            o_masks = [go >= float(g) for g in range(1, 8)]
            lanes = slice(i * PB, (i + 1) * PB)
            for f in range(4):
                base = f * LEV
                e = horiz[base:base + 8, lanes]
                o = horiz[base + 64:base + 72, lanes]
                for g in range(1, 8):
                    e = jnp.where(e_masks[g - 1], horiz[base + 8 * g:base + 8 * g + 8, lanes], e)
                    o = jnp.where(o_masks[g - 1], horiz[base + 64 + 8 * g:base + 72 + 8 * g, lanes], o)
                val_ref[f, c:c + 1, :] = jnp.sum(e * we + o * wo, axis=0, keepdims=True)
    if before is not None:
        return moved, bin_rows(b_low, b_lo, b_hi, before[4])


def last_group(before, east):
    moved, low, lo, hi = move(*before, east)
    return moved, bin_rows(low, lo, hi, before[4])


def solve(ends, binned, upper_ref, lower_ref, inv_ref, rhs_ref, fwd_ref, back_ref, out_ref):
    top, bot = ends
    half = LEV // 2
    inv = inv_ref[...]
    u, low = upper_ref[...], lower_ref[...]
    upper_rows = lax.broadcasted_iota(jnp.int32, (LEV, COLS), 0) < half
    rhs_ref[...] = binned * inv
    fwd_ref[...] = jnp.where(upper_rows, low, u) * inv
    back_ref[...] = jnp.where(upper_rows, u, low) * inv
    d = rhs_ref[0:1, :]
    e = rhs_ref[LEV - 1:LEV, :]
    ds, es = [d], [e]
    for k in range(1, half):
        m = LEV - 1 - k
        d = rhs_ref[k:k + 1, :] + fwd_ref[k:k + 1, :] * d
        e = rhs_ref[m:m + 1, :] + fwd_ref[m:m + 1, :] * e
        ds.append(d)
        es.append(e)
    kappa = upper_ref[half - 1:half, :]
    alpha = back_ref[half - 1:half, :]
    beta = back_ref[half:half + 1, :]
    det = (kappa * (top + bot) + top * bot) * inv_ref[half - 1:half, :] * inv_ref[half:half + 1, :]
    x = (d + alpha * e) / det
    y = e + beta * x
    out_ref[half - 1:half, :] = x
    out_ref[half:half + 1, :] = y
    for k in range(half - 2, -1, -1):
        m = LEV - 1 - k
        x = ds[k] + back_ref[k:k + 1, :] * x
        y = es[k] + back_ref[m:m + 1, :] * y
        out_ref[k:k + 1, :] = x
        out_ref[m:m + 1, :] = y


N_BAND = 8
N_TILE = 32
NY, NZ = 4, 8
B_DEV = 160
AHEAD = 5
SUB = LEV // N_BAND
ROWS = 32


def offset(i):
    j = (i + NY) // (2 * NY)
    r = (i + NY) % (2 * NY)
    dy = (1 - (j + 7) // 8) * (r % NY) + ((j + 7) // 8) * (r // 2)
    dz = (j + (r % 2) * (NZ - 2 * j)) % NZ
    dz = dz * (1 - j // 4) + 4 * (j // 4)
    dy = dy * (1 - j // 4) + (j // 4) * (r % NY)
    return dy, dz


def place(tile, i, sign):
    dy, dz = offset(i)
    y = (tile // NZ + NY + sign * dy) % NY
    z = (tile % NZ + NZ + sign * dz) % NZ
    return y * NZ + z


def build(dest_ref, parts, col_ref, send_f, send_c):
    dest = dest_ref[...].astype(F32)
    wide = jnp.broadcast_to(dest, (B_DEV, B_DEV))
    row = lax.broadcasted_iota(jnp.int32, (B_DEV, B_DEV), 0)
    lane = lax.broadcasted_iota(jnp.int32, (B_DEV, B_DEV), 1)
    tall = jnp.sum(jnp.where(row == lane, wide, 0.0), axis=1, keepdims=True)
    same = jnp.where((tall == wide) & (row < lane), 1.0, 0.0)
    rank = jnp.sum(same, axis=0, keepdims=True)
    slots = N_TILE * CAP
    pick = jnp.where(iota((slots, B_DEV), 0) == dest * CAP + rank, 1.0, 0.0).astype(BF)
    for f, ref in enumerate(parts[:3]):
        x = ref[...]
        hi = x.astype(BF)
        rest = x - hi.astype(F32)
        mid = rest.astype(BF)
        low = (rest - mid.astype(F32)).astype(BF)
        total = jnp.dot(pick, hi, preferred_element_type=F32)
        total = total + jnp.dot(pick, mid, preferred_element_type=F32)
        total = total + jnp.dot(pick, low, preferred_element_type=F32)
        for t in range(N_TILE):
            send_f[t * ROWS + f * CAP:t * ROWS + (f + 1) * CAP, :] = total[t * CAP:(t + 1) * CAP]
    mass = parts[3][...].astype(BF)
    total = jnp.dot(pick, mass, preferred_element_type=F32)
    for t in range(N_TILE):
        for r in range(2):
            at = t * CAP + 6 + 2 * r
            send_f[t * ROWS + 30 + r:t * ROWS + 31 + r, :] = total[at:at + 1] * 1024.0 + total[at + 1:at + 2]
    rows = iota((N_TILE * 16, B_DEV), 0)
    place16 = dest * 16 + rank
    pick = jnp.where(rows == place16, 1.0, 0.0).astype(BF)
    both = jnp.dot(pick, col_ref[...].astype(F32).astype(BF), preferred_element_type=F32)
    pick = jnp.where(rows == jnp.where(rank < 6.0, place16 + 10.0, -1.0), 1.0, 0.0).astype(BF)
    both = both + jnp.dot(pick, mass, preferred_element_type=F32)
    send_c[...] = both.astype(BF).reshape(N_TILE, 16, PB)


def kernel(wind, temp, diff, removal, frac, height, noise, mass, column, dest,
           conc_ref, moved_ref,
           table, tperm, east_out, east_in, send_f, send_c, recv_f, recv_c,
           in_f, in_c, in_d, val, val_old, binned, upper, lower, inv, rhs, fwd, back,
           field_send, field_recv, own_sem, in_sem, east_sems, f_send, f_recv, c_send, c_recv):
    band, tile = lax.axis_index("band"), lax.axis_index("tile")
    barrier = pltpu.get_barrier_semaphore()

    def greet_tile(i, _):
        pl.semaphore_signal(barrier, inc=1, device_id=(band, place(tile, i, 1)), device_id_type=pl.DeviceIdType.MESH)
        return 0

    def greet_band(i, _):
        pl.semaphore_signal(barrier, inc=1, device_id=((band + i) % N_BAND, tile), device_id_type=pl.DeviceIdType.MESH)
        return 0

    loads = [pltpu.make_async_copy(ref, in_f.at[f], in_sem.at[f]) for f, ref in enumerate((frac, height, noise, mass))]
    loads.append(pltpu.make_async_copy(column, in_c, in_sem.at[4]))
    loads.append(pltpu.make_async_copy(dest, in_d, in_sem.at[5]))
    for copy in loads:
        copy.start()
    lax.fori_loop(1, N_TILE, greet_tile, 0)
    lax.fori_loop(1, N_BAND, greet_band, 0)
    fields = (wind, temp, diff, removal)
    own = [pltpu.make_async_copy(ref.at[band], table.at[pl.ds(pl.multiple_of(f * LEV + band * SUB, SUB), SUB)], own_sem.at[f])
           for f, ref in enumerate(fields)]
    for copy in own:
        copy.start()
    for copy in loads:
        copy.wait()
    build(in_d, [in_f.at[f] for f in range(4)], in_c, send_f, send_c)
    pl.semaphore_wait(barrier, N_TILE + N_BAND - 2)

    def field_copy(i, f, to, rows_of):
        return pltpu.make_async_remote_copy(
            src_ref=fields[f].at[to], dst_ref=table.at[pl.ds(pl.multiple_of(f * LEV + rows_of * SUB, SUB), SUB)],
            send_sem=field_send.at[i, f], recv_sem=field_recv.at[i, f],
            device_id=(to, tile), device_id_type=pl.DeviceIdType.MESH)

    def record_copies(i):
        to = place(tile, i, 1)
        return [pltpu.make_async_remote_copy(
            src_ref=send_f.at[pl.ds(pl.multiple_of(to * ROWS, 8), ROWS)], dst_ref=recv_f.at[i // G, pl.ds(pl.multiple_of(i % G * ROWS, 8), ROWS)],
            send_sem=f_send.at[i], recv_sem=f_recv.at[i],
            device_id=(band, to), device_id_type=pl.DeviceIdType.MESH),
            pltpu.make_async_remote_copy(
            src_ref=send_c.at[to], dst_ref=recv_c.at[i],
            send_sem=c_send.at[i], recv_sem=c_recv.at[i],
            device_id=(band, to), device_id_type=pl.DeviceIdType.MESH)]

    def send_fields(i, _):
        to = (band + i) % N_BAND
        for f in range(4):
            field_copy(i, f, to, band).start()
        return 0

    def send_records(i, _):
        for copy in record_copies(i):
            copy.start()
        return 0

    lax.fori_loop(1, N_BAND, send_fields, 0)
    lax.fori_loop(1, AHEAD * G, send_records, 0)
    recv_f[0, 0:ROWS, :] = send_f[pl.ds(pl.multiple_of(tile * ROWS, 8), ROWS), :]
    recv_c[0] = send_c[tile]
    binned[...] = jnp.zeros_like(binned)
    for copy in own:
        copy.wait()

    def take_fields(i, _):
        source = (band + N_BAND - i) % N_BAND
        for f in range(4):
            field_copy(i, f, (band + i) % N_BAND, source).wait_recv()
        return 0

    lax.fori_loop(1, N_BAND, take_fields, 0)
    first = jnp.where(lax.broadcasted_iota(jnp.int32, (8, COLS), 1) == 0, 1.0, 0.0).astype(BF)
    east_out[...] = lax.dot_general(first, table[...], (((1,), (1,)), ((), ())), preferred_element_type=F32)
    west = (tile + N_TILE - 1) % N_TILE
    east_copy = pltpu.make_async_remote_copy(
        src_ref=east_out, dst_ref=east_in, send_sem=east_sems.at[0], recv_sem=east_sems.at[1],
        device_id=(band, west), device_id_type=pl.DeviceIdType.MESH)
    east_copy.start()
    split_levels(table, tperm)
    set_kappa(table, upper, lower)
    def take_records(i, _):
        for copy in record_copies(i):
            copy.wait_recv()
        return 0

    def rows_of(q):
        return [jnp.concatenate([recv_f[q, j * ROWS + f * CAP:j * ROWS + (f + 1) * CAP, :] for j in range(G)], axis=0)
                for f in range(3)]

    def col_of(q):
        return jnp.concatenate([recv_c[q * G + j].astype(F32)[:CAP] for j in range(G)], axis=0)

    def mass_of(q):
        out = []
        for j in range(G):
            out.append(recv_c[q * G + j].astype(F32)[CAP:])
            for r in range(2):
                pair = recv_f[q, j * ROWS + 30 + r:j * ROWS + 31 + r, :]
                even = jnp.floor(pair * 0.25) * (1.0 / 256.0)
                out += [even, pair - even * 1024.0]
        return jnp.concatenate(out, axis=0)

    def before_of(q):
        return (*rows_of(q), mass_of(q), col_of(q), [val_old[f] for f in range(4)])

    def put(q, moved):
        for j in range(G):
            moved_ref[pl.ds(place(tile, q * G + j, -1) * CAP, CAP), :] = moved[j * CAP:(j + 1) * CAP]

    lax.fori_loop(1, G, take_records, 0)
    one = jnp.ones((1, COLS), F32)
    carry = pivots(0, (one, one), upper, lower, inv)
    fr, h, _ = rows_of(0)
    group_work((fr, h, col_of(0)), None, tperm, val_old, None)
    east_copy.wait()
    east = [east_in[:, f * LEV:(f + 1) * LEV] for f in range(4)]

    def body(q, carry):
        first = jnp.minimum((q + AHEAD - 1) * G, N_TILE)
        lax.fori_loop(first, jnp.minimum(first + G, N_TILE), send_records, 0)
        lax.fori_loop(q * G, q * G + G, take_records, 0)
        carry, ends = pivots(q, carry[0], upper, lower, inv)
        fr, h, _ = rows_of(q)
        moved, bins = group_work((fr, h, col_of(q)), before_of(q - 1), tperm, val, east)
        put(q - 1, moved)
        binned[...] += bins
        val_old[...] = val[...]
        return carry, ends

    _, ends = lax.fori_loop(1, NG, body, carry)
    moved, bins = last_group(before_of(NG - 1), east)
    put(NG - 1, moved)
    solve(ends, binned[...] + bins, upper, lower, inv, rhs, fwd, back, conc_ref)

    def sent_fields(i, _):
        for f in range(4):
            field_copy(i, f, (band + i) % N_BAND, band).wait_send()
        return 0

    def sent_records(i, _):
        for copy in record_copies(i):
            copy.wait_send()
        return 0

    lax.fori_loop(1, N_BAND, sent_fields, 0)
    lax.fori_loop(1, N_TILE, sent_records, 0)


def hand_on(conc_in, moved_in, conc_out, moved_out, conc, moved, sem):
    ins = [pltpu.make_async_copy(moved_in, moved, sem.at[0]), pltpu.make_async_copy(conc_in, conc, sem.at[1])]
    outs = [pltpu.make_async_copy(moved, moved_out, sem.at[2]), pltpu.make_async_copy(conc, conc_out, sem.at[3])]
    for copy in ins:
        copy.start()
    for before, after in zip(ins, outs):
        before.wait()
        after.start()
    for copy in outs:
        copy.wait()


def shards(wind, temp, diff, removal, frac, height, mass, noise, column, dest):
    vm = pl.BlockSpec(memory_space=pltpu.VMEM)
    hbm = pl.BlockSpec(memory_space=pltpu.HBM)
    grid = pltpu.VMEM((LEV, COLS), F32)
    dma = pltpu.SemaphoreType.DMA
    conc, moved = pl.pallas_call(
        kernel,
        out_shape=(jax.ShapeDtypeStruct((LEV, COLS), F32), jax.ShapeDtypeStruct((N_TILE * CAP, PB), F32)),
        in_specs=[hbm] * 10,
        out_specs=(vm, vm),
        scratch_shapes=[
            pltpu.VMEM((4 * LEV, COLS), BF), pltpu.VMEM((4 * LEV, COLS), BF),
            pltpu.VMEM((8, 4 * LEV), F32), pltpu.VMEM((8, 4 * LEV), F32),
            pltpu.VMEM((N_TILE * ROWS, PB), F32), pltpu.VMEM((N_TILE, 16, PB), BF),
            pltpu.VMEM((NG, G * ROWS, PB), F32), pltpu.VMEM((N_TILE, 16, PB), BF),
            pltpu.VMEM((4, B_DEV, PB), F32), pltpu.VMEM((B_DEV, PB), jnp.int32), pltpu.VMEM((1, B_DEV), jnp.int32),
            pltpu.VMEM((4, R, PB), F32), pltpu.VMEM((4, R, PB), F32), grid,
            grid, grid, grid, grid, grid, grid,
            dma((N_BAND, 4)), dma((N_BAND, 4)), dma((4,)), dma((6,)), dma((2,)),
            dma((N_TILE,)), dma((N_TILE,)), dma((N_TILE,)), dma((N_TILE,)),
        ],
        compiler_params=pltpu.CompilerParams(
            collective_id=0, has_side_effects=True, vmem_limit_bytes=63 * 2**20),
        cost_estimate=pl.CostEstimate(flops=2 * 40960 * 256 * 640, bytes_accessed=2 * 2**20, transcendentals=0),
    )(wind, temp, diff, removal, frac, height, noise, mass, column, dest.reshape(1, B_DEV))
    conc, moved = pl.pallas_call(
        hand_on,
        out_shape=(jax.ShapeDtypeStruct((LEV, COLS), F32), jax.ShapeDtypeStruct((N_TILE * CAP, PB), F32)),
        in_specs=[hbm] * 2, out_specs=(hbm, hbm),
        scratch_shapes=[grid, pltpu.VMEM((N_TILE * CAP, PB), F32), dma((4,))],
        compiler_params=pltpu.CompilerParams(vmem_limit_bytes=63 * 2**20),
    )(conc, moved)
    return conc[None], moved


def solution(mesh):
    read = P(None, "band", "tile")
    rec = P(("band", "tile"), None)
    return jax.shard_map(
        shards, mesh=mesh,
        in_specs=(read,) * 4 + (rec,) * 5 + (P(("band", "tile")),),
        out_specs=(P("band", None, "tile"), rec), check_vma=False)
```

```python
import jax
import jax.numpy as jnp
from jax import lax
from jax.experimental import pallas as pl
from jax.experimental.pallas import tpu as pltpu
from jax.sharding import PartitionSpec as P

LEV = 128
COLS = 256
CAP = 10
PB = 128
CH = 2
F32 = jnp.float32
BF = jnp.bfloat16


def iota(shape, dim, dtype=F32):
    return lax.broadcasted_iota(jnp.int32, shape, dim).astype(dtype)


def split_levels(table_ref, tperm_ref):
    row = lax.broadcasted_iota(jnp.int32, (LEV, LEV), 0)
    col = lax.broadcasted_iota(jnp.int32, (LEV, LEV), 1)
    source = jnp.where(row < LEV // 2, 2 * row, 2 * row - (LEV - 1))
    perm = (col == source).astype(F32).astype(BF)
    for f in range(4):
        part = pl.ds(f * LEV, LEV)
        tperm_ref[part, :] = jnp.dot(perm, table_ref[part, :], preferred_element_type=F32).astype(BF)


def set_kappa(table_ref, upper_ref, lower_ref):
    k = table_ref[pl.ds(2 * LEV, LEV), :].astype(F32)
    kappa = 0.5 * (k[:-1] + k[1:])
    zero = jnp.zeros((1, COLS), F32)
    upper_ref[...] = jnp.concatenate([kappa, zero], axis=0)
    lower_ref[...] = jnp.concatenate([zero, kappa], axis=0)


def pivots(step, carry, upper_ref, lower_ref, inv_ref):
    top, bot = carry
    for i in range(LEV // 2 // NG):
        k = LEV // 2 // NG * step + i
        u = upper_ref[pl.ds(k, 1), :]
        inv = 1.0 / (top + u)
        inv_ref[pl.ds(k, 1), :] = inv
        last_top = top
        top = 1.0 + u * (top * inv)
        m = LEV - 1 - k
        low = lower_ref[pl.ds(m, 1), :]
        inv = 1.0 / (bot + low)
        inv_ref[pl.ds(m, 1), :] = inv
        last_bot = bot
        bot = 1.0 + low * (bot * inv)
    return (top, bot), (last_top, last_bot)


G = 4
NG = 8
R = G * CAP


def spread(x, c, rows, dtype=F32):
    return jnp.broadcast_to(x[c:c + 1], (rows, PB)).astype(dtype)


def move(fr, height, noise, mass, col, val, east):
    low = jnp.clip(jnp.floor(height), 0.0, LEV - 2.0)
    fz = height - low
    right = fr.astype(BF).astype(F32)
    edge = jnp.where(col == COLS - 1.0, right, 0.0)
    low_i = low.astype(jnp.int32)

    def picked(table, index):
        return jnp.concatenate([jnp.take_along_axis(table, index[r:r + 8], axis=1) for r in range(0, R, 8)], axis=0)

    w, temp, kd, rate = [
        val[f] + edge * (picked(east[f], low_i) * (1.0 - fz) + picked(east[f], low_i + 1) * fz) for f in range(4)]
    znew = jnp.clip(height + w + jnp.sqrt(2.0 * kd) * noise, 0.0, LEV - 1.0)
    moved = jnp.where(mass > 0, znew, 0.0)
    load = mass * jnp.exp(-rate) * temp
    low = jnp.clip(jnp.floor(znew), 0.0, LEV - 2.0)
    fz = znew - low
    return moved, low, load * (1.0 - fz), load * fz


def load_rows(low, load_lo, load_hi, c):
    lev = iota((LEV, PB), 0, BF)
    a = spread(load_lo, c, LEV, BF)
    b = spread(load_hi, c, LEV, BF)
    rest = jnp.where(lev == spread(low + 1.0, c, LEV, BF), b, jnp.zeros_like(b))
    return jnp.where(lev == spread(low, c, LEV, BF), a, rest)


def bin_rows(low, load_lo, load_hi, col):
    loads = jnp.concatenate([load_rows(low, load_lo, load_hi, c) for c in range(R)], axis=1)
    turned = jnp.concatenate([col, jnp.zeros((PB - R, PB), F32)], axis=0).T.astype(BF)
    lanes = iota((PB, COLS), 1, BF)
    one = jnp.ones((PB, COLS), BF)
    picks = jnp.concatenate(
        [jnp.where(lanes == jnp.broadcast_to(turned[:, c:c + 1], (PB, COLS)), one, jnp.zeros_like(one)) for c in range(R)],
        axis=0)
    return jnp.dot(loads, picks, preferred_element_type=F32)


def group_work(now, before, tperm_ref, val_ref, east):
    fr, height, col = now
    if before is not None:
        moved, b_low, b_lo, b_hi = move(*before, east)
    left = 1.0 - fr
    low = jnp.clip(jnp.floor(height), 0.0, LEV - 2.0)
    odd_i = jnp.floor(low * 0.5)
    even_i = jnp.floor((low + 1.0) * 0.5)
    w_even = jnp.maximum(0.0, 1.0 - jnp.abs(height - 2.0 * even_i))
    w_odd = jnp.maximum(0.0, 1.0 - jnp.abs(height - (2.0 * odd_i + 1.0)))
    g_even = jnp.floor(even_i * 0.125)
    g_odd = jnp.floor(odd_i * 0.125)
    s_even = even_i - 8.0 * g_even
    s_odd = odd_i - 8.0 * g_odd
    col1 = col + 1.0
    ids = iota((COLS, PB), 0, BF)
    sub = iota((8, PB), 0)
    zero = jnp.zeros((COLS, PB), BF)
    for c0 in range(0, R, CH):
        weights = []
        for c in range(c0, c0 + CH):
            rest = jnp.where(ids == spread(col1, c, COLS, BF), spread(fr, c, COLS, BF), zero)
            weights.append(jnp.where(ids == spread(col, c, COLS, BF), spread(left, c, COLS, BF), rest))
        horiz = jnp.dot(tperm_ref[...], jnp.concatenate(weights, axis=1), preferred_element_type=F32)
        for i in range(CH):
            c = c0 + i
            ge = spread(g_even, c, 8)
            go = spread(g_odd, c, 8)
            we = jnp.where(sub == spread(s_even, c, 8), spread(w_even, c, 8), 0.0)
            wo = jnp.where(sub == spread(s_odd, c, 8), spread(w_odd, c, 8), 0.0)
            e_masks = [ge >= float(g) for g in range(1, 8)]
            o_masks = [go >= float(g) for g in range(1, 8)]
            lanes = slice(i * PB, (i + 1) * PB)
            for f in range(4):
                base = f * LEV
                e = horiz[base:base + 8, lanes]
                o = horiz[base + 64:base + 72, lanes]
                for g in range(1, 8):
                    e = jnp.where(e_masks[g - 1], horiz[base + 8 * g:base + 8 * g + 8, lanes], e)
                    o = jnp.where(o_masks[g - 1], horiz[base + 64 + 8 * g:base + 72 + 8 * g, lanes], o)
                val_ref[f, c:c + 1, :] = jnp.sum(e * we + o * wo, axis=0, keepdims=True)
    if before is not None:
        return moved, bin_rows(b_low, b_lo, b_hi, before[4])


def last_group(before, east):
    moved, low, lo, hi = move(*before, east)
    return moved, bin_rows(low, lo, hi, before[4])


def solve(ends, binned, upper_ref, lower_ref, inv_ref, rhs_ref, fwd_ref, back_ref, out_ref):
    top, bot = ends
    half = LEV // 2
    inv = inv_ref[...]
    u, low = upper_ref[...], lower_ref[...]
    upper_rows = lax.broadcasted_iota(jnp.int32, (LEV, COLS), 0) < half
    rhs_ref[...] = binned * inv
    fwd_ref[...] = jnp.where(upper_rows, low, u) * inv
    back_ref[...] = jnp.where(upper_rows, u, low) * inv
    d = rhs_ref[0:1, :]
    e = rhs_ref[LEV - 1:LEV, :]
    ds, es = [d], [e]
    for k in range(1, half):
        m = LEV - 1 - k
        d = rhs_ref[k:k + 1, :] + fwd_ref[k:k + 1, :] * d
        e = rhs_ref[m:m + 1, :] + fwd_ref[m:m + 1, :] * e
        ds.append(d)
        es.append(e)
    kappa = upper_ref[half - 1:half, :]
    alpha = back_ref[half - 1:half, :]
    beta = back_ref[half:half + 1, :]
    det = (kappa * (top + bot) + top * bot) * inv_ref[half - 1:half, :] * inv_ref[half:half + 1, :]
    x = (d + alpha * e) / det
    y = e + beta * x
    out_ref[half - 1:half, :] = x
    out_ref[half:half + 1, :] = y
    for k in range(half - 2, -1, -1):
        m = LEV - 1 - k
        x = ds[k] + back_ref[k:k + 1, :] * x
        y = es[k] + back_ref[m:m + 1, :] * y
        out_ref[k:k + 1, :] = x
        out_ref[m:m + 1, :] = y


N_BAND = 8
N_TILE = 32
NY, NZ = 4, 8
B_DEV = 160
AHEAD = 5
SUB = LEV // N_BAND
ROWS = 32


def offset(i):
    j = (i + NY) // (2 * NY)
    r = (i + NY) % (2 * NY)
    dy = (1 - (j + 7) // 8) * (r % NY) + ((j + 7) // 8) * (r // 2)
    dz = (j + (r % 2) * (NZ - 2 * j)) % NZ
    dz = dz * (1 - j // 4) + 4 * (j // 4)
    dy = dy * (1 - j // 4) + (j // 4) * (r % NY)
    return dy, dz


def place(tile, i, sign):
    dy, dz = offset(i)
    y = (tile // NZ + NY + sign * dy) % NY
    z = (tile % NZ + NZ + sign * dz) % NZ
    return y * NZ + z


def build(dest_ref, parts, col_ref, send_f, send_c):
    dest = dest_ref[...].astype(F32)
    wide = jnp.broadcast_to(dest, (B_DEV, B_DEV))
    row = lax.broadcasted_iota(jnp.int32, (B_DEV, B_DEV), 0)
    lane = lax.broadcasted_iota(jnp.int32, (B_DEV, B_DEV), 1)
    tall = jnp.sum(jnp.where(row == lane, wide, 0.0), axis=1, keepdims=True)
    same = jnp.where((tall == wide) & (row < lane), 1.0, 0.0)
    rank = jnp.sum(same, axis=0, keepdims=True)
    slots = N_TILE * CAP
    pick = jnp.where(iota((slots, B_DEV), 0) == dest * CAP + rank, 1.0, 0.0).astype(BF)
    for f, ref in enumerate(parts[:3]):
        x = ref[...]
        hi = x.astype(BF)
        rest = x - hi.astype(F32)
        mid = rest.astype(BF)
        low = (rest - mid.astype(F32)).astype(BF)
        total = jnp.dot(pick, hi, preferred_element_type=F32)
        total = total + jnp.dot(pick, mid, preferred_element_type=F32)
        total = total + jnp.dot(pick, low, preferred_element_type=F32)
        for t in range(N_TILE):
            send_f[t * ROWS + f * CAP:t * ROWS + (f + 1) * CAP, :] = total[t * CAP:(t + 1) * CAP]
    mass = parts[3][...].astype(BF)
    total = jnp.dot(pick, mass, preferred_element_type=F32)
    for t in range(N_TILE):
        for r in range(2):
            at = t * CAP + 6 + 2 * r
            send_f[t * ROWS + 30 + r:t * ROWS + 31 + r, :] = total[at:at + 1] * 1024.0 + total[at + 1:at + 2]
    rows = iota((N_TILE * 16, B_DEV), 0)
    place16 = dest * 16 + rank
    pick = jnp.where(rows == place16, 1.0, 0.0).astype(BF)
    both = jnp.dot(pick, col_ref[...].astype(F32).astype(BF), preferred_element_type=F32)
    pick = jnp.where(rows == jnp.where(rank < 6.0, place16 + 10.0, -1.0), 1.0, 0.0).astype(BF)
    both = both + jnp.dot(pick, mass, preferred_element_type=F32)
    send_c[...] = both.astype(BF).reshape(N_TILE, 16, PB)


def kernel(wind, temp, diff, removal, frac, height, noise, mass, column, dest,
           conc_ref, moved_ref,
           table, tperm, east_out, east_in, send_f, send_c, recv_f, recv_c,
           in_f, in_c, in_d, val, val_old, binned, upper, lower, inv, rhs, fwd, back,
           field_send, field_recv, own_sem, in_sem, east_sems, f_send, f_recv, c_send, c_recv):
    band, tile = lax.axis_index("band"), lax.axis_index("tile")
    barrier = pltpu.get_barrier_semaphore()

    def greet_tile(i, _):
        pl.semaphore_signal(barrier, inc=1, device_id=(band, place(tile, i, 1)), device_id_type=pl.DeviceIdType.MESH)
        return 0

    def greet_band(i, _):
        pl.semaphore_signal(barrier, inc=1, device_id=((band + i) % N_BAND, tile), device_id_type=pl.DeviceIdType.MESH)
        return 0

    loads = [pltpu.make_async_copy(ref, in_f.at[f], in_sem.at[f]) for f, ref in enumerate((frac, height, noise, mass))]
    loads.append(pltpu.make_async_copy(column, in_c, in_sem.at[4]))
    loads.append(pltpu.make_async_copy(dest, in_d, in_sem.at[5]))
    for copy in loads:
        copy.start()
    lax.fori_loop(1, N_TILE, greet_tile, 0)
    lax.fori_loop(1, N_BAND, greet_band, 0)
    fields = (wind, temp, diff, removal)
    own = [pltpu.make_async_copy(ref.at[band], table.at[pl.ds(pl.multiple_of(f * LEV + band * SUB, SUB), SUB)], own_sem.at[f])
           for f, ref in enumerate(fields)]
    for copy in own:
        copy.start()
    for copy in loads:
        copy.wait()
    build(in_d, [in_f.at[f] for f in range(4)], in_c, send_f, send_c)
    pl.semaphore_wait(barrier, N_TILE + N_BAND - 2)

    def field_copy(i, f, to, rows_of):
        return pltpu.make_async_remote_copy(
            src_ref=fields[f].at[to], dst_ref=table.at[pl.ds(pl.multiple_of(f * LEV + rows_of * SUB, SUB), SUB)],
            send_sem=field_send.at[i, f], recv_sem=field_recv.at[i, f],
            device_id=(to, tile), device_id_type=pl.DeviceIdType.MESH)

    def record_copies(i):
        to = place(tile, i, 1)
        return [pltpu.make_async_remote_copy(
            src_ref=send_f.at[pl.ds(pl.multiple_of(to * ROWS, 8), ROWS)], dst_ref=recv_f.at[i // G, pl.ds(pl.multiple_of(i % G * ROWS, 8), ROWS)],
            send_sem=f_send.at[i], recv_sem=f_recv.at[i],
            device_id=(band, to), device_id_type=pl.DeviceIdType.MESH),
            pltpu.make_async_remote_copy(
            src_ref=send_c.at[to], dst_ref=recv_c.at[i],
            send_sem=c_send.at[i], recv_sem=c_recv.at[i],
            device_id=(band, to), device_id_type=pl.DeviceIdType.MESH)]

    def send_fields(i, _):
        to = (band + i) % N_BAND
        for f in range(4):
            field_copy(i, f, to, band).start()
        return 0

    def send_records(i, _):
        for copy in record_copies(i):
            copy.start()
        return 0

    lax.fori_loop(1, N_BAND, send_fields, 0)
    lax.fori_loop(1, AHEAD * G, send_records, 0)
    recv_f[0, 0:ROWS, :] = send_f[pl.ds(pl.multiple_of(tile * ROWS, 8), ROWS), :]
    recv_c[0] = send_c[tile]
    binned[...] = jnp.zeros_like(binned)
    for copy in own:
        copy.wait()

    def take_fields(i, _):
        source = (band + N_BAND - i) % N_BAND
        for f in range(4):
            field_copy(i, f, (band + i) % N_BAND, source).wait_recv()
        return 0

    lax.fori_loop(1, N_BAND, take_fields, 0)
    first = jnp.where(lax.broadcasted_iota(jnp.int32, (8, COLS), 1) == 0, 1.0, 0.0).astype(BF)
    east_out[...] = lax.dot_general(first, table[...], (((1,), (1,)), ((), ())), preferred_element_type=F32)
    west = (tile + N_TILE - 1) % N_TILE
    east_copy = pltpu.make_async_remote_copy(
        src_ref=east_out, dst_ref=east_in, send_sem=east_sems.at[0], recv_sem=east_sems.at[1],
        device_id=(band, west), device_id_type=pl.DeviceIdType.MESH)
    east_copy.start()
    split_levels(table, tperm)
    set_kappa(table, upper, lower)
    def sent_fields(i, _):
        for f in range(4):
            field_copy(i, f, (band + i) % N_BAND, band).wait_send()
        return 0

    def sent_records(i, _):
        for copy in record_copies(i):
            copy.wait_send()
        return 0

    def take_records(i, _):
        for copy in record_copies(i):
            copy.wait_recv()
        return 0

    def rows_of(q):
        return [jnp.concatenate([recv_f[q, j * ROWS + f * CAP:j * ROWS + (f + 1) * CAP, :] for j in range(G)], axis=0)
                for f in range(3)]

    def col_of(q):
        return jnp.concatenate([recv_c[q * G + j].astype(F32)[:CAP] for j in range(G)], axis=0)

    def mass_of(q):
        out = []
        for j in range(G):
            out.append(recv_c[q * G + j].astype(F32)[CAP:])
            for r in range(2):
                pair = recv_f[q, j * ROWS + 30 + r:j * ROWS + 31 + r, :]
                even = jnp.floor(pair * 0.25) * (1.0 / 256.0)
                out += [even, pair - even * 1024.0]
        return jnp.concatenate(out, axis=0)

    def before_of(q):
        return (*rows_of(q), mass_of(q), col_of(q), [val_old[f] for f in range(4)])

    def put(q, moved):
        for j in range(G):
            moved_ref[pl.ds(place(tile, q * G + j, -1) * CAP, CAP), :] = moved[j * CAP:(j + 1) * CAP]

    lax.fori_loop(1, N_BAND, sent_fields, 0)
    lax.fori_loop(1, G, take_records, 0)
    one = jnp.ones((1, COLS), F32)
    carry = pivots(0, (one, one), upper, lower, inv)
    fr, h, _ = rows_of(0)
    group_work((fr, h, col_of(0)), None, tperm, val_old, None)
    east_copy.wait()
    east = [east_in[:, f * LEV:(f + 1) * LEV] for f in range(4)]

    def body(q, carry):
        lax.fori_loop(jnp.maximum((q - 1) * G, 1), q * G, sent_records, 0)
        lax.fori_loop(q * G, q * G + G, take_records, 0)
        first = jnp.minimum((q + AHEAD - 1) * G, N_TILE)
        lax.fori_loop(first, jnp.minimum(first + G, N_TILE), send_records, 0)
        carry, ends = pivots(q, carry[0], upper, lower, inv)
        fr, h, _ = rows_of(q)
        moved, bins = group_work((fr, h, col_of(q)), before_of(q - 1), tperm, val, east)
        put(q - 1, moved)
        binned[...] += bins
        val_old[...] = val[...]
        return carry, ends

    _, ends = lax.fori_loop(1, NG, body, carry)
    moved, bins = last_group(before_of(NG - 1), east)
    put(NG - 1, moved)
    solve(ends, binned[...] + bins, upper, lower, inv, rhs, fwd, back, conc_ref)

    lax.fori_loop((NG - 1) * G, N_TILE, sent_records, 0)


def hand_on(conc_in, moved_in, conc_out, moved_out, conc, moved, sem):
    ins = [pltpu.make_async_copy(moved_in, moved, sem.at[0]), pltpu.make_async_copy(conc_in, conc, sem.at[1])]
    outs = [pltpu.make_async_copy(moved, moved_out, sem.at[2]), pltpu.make_async_copy(conc, conc_out, sem.at[3])]
    for copy in ins:
        copy.start()
    for before, after in zip(ins, outs):
        before.wait()
        after.start()
    for copy in outs:
        copy.wait()


def shards(wind, temp, diff, removal, frac, height, mass, noise, column, dest):
    vm = pl.BlockSpec(memory_space=pltpu.VMEM)
    hbm = pl.BlockSpec(memory_space=pltpu.HBM)
    grid = pltpu.VMEM((LEV, COLS), F32)
    dma = pltpu.SemaphoreType.DMA
    conc, moved = pl.pallas_call(
        kernel,
        out_shape=(jax.ShapeDtypeStruct((LEV, COLS), F32), jax.ShapeDtypeStruct((N_TILE * CAP, PB), F32)),
        in_specs=[hbm] * 10,
        out_specs=(vm, vm),
        scratch_shapes=[
            pltpu.VMEM((4 * LEV, COLS), BF), pltpu.VMEM((4 * LEV, COLS), BF),
            pltpu.VMEM((8, 4 * LEV), F32), pltpu.VMEM((8, 4 * LEV), F32),
            pltpu.VMEM((N_TILE * ROWS, PB), F32), pltpu.VMEM((N_TILE, 16, PB), BF),
            pltpu.VMEM((NG, G * ROWS, PB), F32), pltpu.VMEM((N_TILE, 16, PB), BF),
            pltpu.VMEM((4, B_DEV, PB), F32), pltpu.VMEM((B_DEV, PB), jnp.int32), pltpu.VMEM((1, B_DEV), jnp.int32),
            pltpu.VMEM((4, R, PB), F32), pltpu.VMEM((4, R, PB), F32), grid,
            grid, grid, grid, grid, grid, grid,
            dma((N_BAND, 4)), dma((N_BAND, 4)), dma((4,)), dma((6,)), dma((2,)),
            dma((N_TILE,)), dma((N_TILE,)), dma((N_TILE,)), dma((N_TILE,)),
        ],
        compiler_params=pltpu.CompilerParams(
            collective_id=0, has_side_effects=True, vmem_limit_bytes=63 * 2**20),
        cost_estimate=pl.CostEstimate(flops=2 * 40960 * 256 * 640, bytes_accessed=2 * 2**20, transcendentals=0),
    )(wind, temp, diff, removal, frac, height, noise, mass, column, dest.reshape(1, B_DEV))
    conc, moved = pl.pallas_call(
        hand_on,
        out_shape=(jax.ShapeDtypeStruct((LEV, COLS), F32), jax.ShapeDtypeStruct((N_TILE * CAP, PB), F32)),
        in_specs=[hbm] * 2, out_specs=(hbm, hbm),
        scratch_shapes=[grid, pltpu.VMEM((N_TILE * CAP, PB), F32), dma((4,))],
        compiler_params=pltpu.CompilerParams(vmem_limit_bytes=63 * 2**20),
    )(conc, moved)
    return conc[None], moved


def solution(mesh):
    read = P(None, "band", "tile")
    rec = P(("band", "tile"), None)
    return jax.shard_map(
        shards, mesh=mesh,
        in_specs=(read,) * 4 + (rec,) * 5 + (P(("band", "tile")),),
        out_specs=(P("band", None, "tile"), rec), check_vma=False)
```
